128 devices in a mesh: ctx: 16 (over z, y_hi, core), head: 8 (over x, y_lo).
Axes of the slice: x: 4, y: 4 (y_hi: 2, y_lo: 2; y = y_hi * 2 + y_lo), z: 4, core: 2. Of those that a mesh axis runs over, the one named last changes fastest.
Arguments:
- hidden_rows: bfloat16 [16384, 5120], P(('ctx', 'head')), may hold values from -6 to 6
- norm_gain: float32 [5120], replicated, may hold values from 0.1 to 1.9
- w_query: bfloat16 [5120, 5120], P(None, 'head'), may hold values from -1 to 1
- w_key: bfloat16 [5120, 1024], P(None, 'head'), may hold values from -1 to 1
- w_value: bfloat16 [5120, 1024], P(None, 'head'), may hold values from -0.078125 to 0.078125
- w_out: bfloat16 [5120, 5120], P('head'), may hold values from -0.078125 to 0.078125
- ancestors: int32 [128, 4], P('ctx'), may hold values from -1 to 126, as said below
Outputs:
- attention_out: bfloat16 [16384, 5120], P(('ctx', 'head'))
The draws below stay inside these ranges and needn't reach their ends.
Inputs may be any that keep to these rules, and one draw needn't show every extreme that they name: `ancestors`: row b lists distinct earlier blocks of the same packed tree as global block numbers, nearest first, then -1 in the remaining slots (entry k + 1 is -1 wherever entry k is); every listed block lies at most 4 * (9) blocks before block b.
All inputs are finite; a program needn't handle non-finite values.
Results may differ from the reference program's by a relative error of at most 0.02.
Values may be sent and summed in bfloat16 or wider, within the bound.
A program may use at most 128 MiB of HBM per device.

```python
import jax
import jax.numpy as jnp
from jax import lax

D = 5120
HEADS = 40
KV_HEADS = 8
HDIM = 128
BLOCK = 128
MAXA = 4
TOK_DEV = 1024
SEQ = 16384
NBLK = 128
BLK_DEV = 8
N_CTX = 16
N_HEAD = 8


def draw_hidden_rows(key, part):
    noise = jax.random.normal(jax.random.fold_in(key, 1), (SEQ, D), jnp.float32)
    return jnp.clip(noise, -6.0, 6.0).astype(jnp.bfloat16)


def draw_w_query(key, part):
    base = jax.random.normal(jax.random.fold_in(key, 21), (D, HEADS * HDIM), jnp.float32) * D ** (-0.5)
    return jnp.clip(base, -1.0, 1.0).astype(jnp.bfloat16)


def draw_w_key(key, part):
    base = jax.random.normal(jax.random.fold_in(key, 22), (D, KV_HEADS * HDIM), jnp.float32) * D ** (-0.5)
    return jnp.clip(base, -1.0, 1.0).astype(jnp.bfloat16)


def draw_ancestors(key, part):
    tree_split = jax.random.randint(jax.random.fold_in(key, 11), (), NBLK // 4, 3 * NBLK // 4 + 1)
    block_index = jnp.arange(NBLK, dtype=jnp.int32)
    tree_start = jnp.where(block_index >= tree_split, tree_split, 0).astype(jnp.int32)
    offsets = jax.random.randint(jax.random.fold_in(key, 12), (NBLK,), 1, BLK_DEV + 2)
    parent = jnp.maximum(block_index - offsets, tree_start)
    parent = jnp.where(block_index == tree_start, -1, parent)
    parent = jnp.where(block_index == NBLK - 1, NBLK - 2, parent).astype(jnp.int32)
    columns = [parent]
    current = parent
    for depth_step in range(MAXA - 1):
        current = jnp.where(current >= 0, parent[jnp.maximum(current, 0)], -1).astype(jnp.int32)
        columns.append(current)
    return jnp.stack(columns, axis=1).astype(jnp.int32)


def block_scale(own_key, shape, pieces, smallest, high):
    factor_of = 1.0
    for dim, blocks in pieces:
        heights = jax.random.uniform(jax.random.fold_in(jax.random.fold_in(own_key, 6), dim), (blocks,), jnp.float32, smallest / len(pieces), high / len(pieces))
        factor_of = factor_of * jnp.repeat(jnp.exp(heights), shape[dim] // blocks).reshape((-1,) + (1,) * (len(shape) - 1 - dim))
    return factor_of


def scatter_about(rng, shape, width, most, pieces=(), kind=jnp.bfloat16):
    array = width * jax.random.normal(rng, shape, jnp.float32)
    if pieces:
        array = array * block_scale(rng, shape, pieces, -0.22, 0.18)
    return jnp.clip(array, -most, most).astype(kind)


def setup_inputs(seed: int = 0) -> dict:
    arg_keys = jax.random.split(jax.random.key(seed), 8)
    hidden_rows = draw_hidden_rows(jax.random.fold_in(arg_keys[7], 71), 0)
    norm_gain = jnp.clip(1.0 + 0.18 * jax.random.normal(arg_keys[1], (D,), jnp.float32), 0.1, 1.9)
    w_query = draw_w_query(jax.random.fold_in(arg_keys[7], 71), 0)
    w_key = draw_w_key(jax.random.fold_in(arg_keys[7], 71), 0)
    w_value = scatter_about(arg_keys[4], (D, KV_HEADS * HDIM), D ** -0.5, 0.078125, ((1, 8),))
    w_out = scatter_about(arg_keys[5], (HEADS * HDIM, D), (HEADS * HDIM) ** -0.5, 0.078125, ((0, 8),))
    ancestors = draw_ancestors(jax.random.fold_in(arg_keys[7], 71), 0)
    return dict(hidden_rows=hidden_rows, norm_gain=norm_gain, w_query=w_query, w_key=w_key, w_value=w_value, w_out=w_out, ancestors=ancestors)


rope_base = 1000000.0

def rotate(tensor, position):
    half_width = tensor.shape[-1] // 2
    frequency = jnp.power(rope_base, -2.0 * jnp.arange(half_width, dtype=jnp.float32) / tensor.shape[-1])
    angles = position[:, None] * frequency[None, :]
    cosine = jnp.cos(angles)[:, None, :]
    sine_part = jnp.sin(angles)[:, None, :]
    first_half = tensor[..., :half_width]
    second = tensor[..., half_width:]
    return jnp.concatenate([first_half * cosine - second * sine_part, second * cosine + first_half * sine_part], axis=-1)

def attend(queries, key_diag, value_diag, key_far, value_far, valid):
    blocks, length, groups, per_group, head_depth = queries.shape
    all_keys = jnp.concatenate([key_diag, key_far], axis=1).astype(jnp.float32)
    all_values = jnp.concatenate([value_diag, value_far], axis=1).astype(jnp.float32)
    scores = jnp.einsum('blgpe,bkge->bgplk', queries.astype(jnp.float32), all_keys, precision=lax.Precision.HIGHEST) * head_depth ** (-0.5)
    causal = lax.broadcasted_iota(jnp.int32, (length, length), 0) >= lax.broadcasted_iota(jnp.int32, (length, length), 1)
    far_ok = jnp.repeat(valid, length, axis=1)
    allowed = jnp.concatenate([jnp.broadcast_to(causal[None], (blocks, length, length)), jnp.broadcast_to(far_ok[:, None, :], (blocks, length, far_ok.shape[1]))], axis=2)
    allowed = allowed[:, None, None, :, :]
    scores = jnp.where(allowed, scores, -1e+30)
    row_max = lax.optimization_barrier(jnp.max(scores, axis=-1, keepdims=True))
    weights = jnp.where(allowed, jnp.exp(scores - row_max), 0.0)
    row_total = lax.optimization_barrier(jnp.sum(weights, axis=-1))
    mixture = jnp.einsum('bgplk,bkge->blgpe', weights, all_values, precision=lax.Precision.HIGHEST)
    return mixture / jnp.transpose(row_total, (0, 3, 1, 2))[..., None]

def reference(hidden_rows, norm_gain, w_query, w_key, w_value, w_out, ancestors):
    as_float = hidden_rows.astype(jnp.float32)
    normed = (as_float * lax.rsqrt(lax.optimization_barrier(jnp.mean(as_float * as_float, axis=1, keepdims=True)) + 1e-06) * norm_gain).astype(jnp.bfloat16)
    queries = jnp.dot(normed, w_query, preferred_element_type=jnp.float32)
    key_rows = jnp.dot(normed, w_key, preferred_element_type=jnp.float32)
    value_rows = jnp.dot(normed, w_value, preferred_element_type=jnp.float32)
    position = jnp.arange(SEQ, dtype=jnp.int32).astype(jnp.float32)
    queries = rotate(queries.reshape(SEQ, HEADS, HDIM), position)
    key_rows = rotate(key_rows.reshape(SEQ, KV_HEADS, HDIM), position)
    per_group = HEADS // KV_HEADS
    key_blocks = key_rows.reshape(NBLK, BLOCK, KV_HEADS, HDIM)
    value_blocks = value_rows.reshape(NBLK, BLOCK, KV_HEADS, HDIM)

    def one_shard(shard_index):
        first_block = (shard_index * BLK_DEV).astype(jnp.int32)
        lists = lax.dynamic_slice_in_dim(ancestors, first_block, BLK_DEV, 0)
        picks = jnp.maximum(lists, 0).reshape(-1)
        far_keys = jnp.take(key_blocks, picks, axis=0).reshape(BLK_DEV, MAXA * BLOCK, KV_HEADS, HDIM)
        far_values = jnp.take(value_blocks, picks, axis=0).reshape(BLK_DEV, MAXA * BLOCK, KV_HEADS, HDIM)
        own_queries = lax.dynamic_slice_in_dim(queries, (first_block * BLOCK).astype(jnp.int32), TOK_DEV, 0)
        own_queries = own_queries.reshape(BLK_DEV, BLOCK, KV_HEADS, per_group, HDIM)
        own_keys = lax.dynamic_slice_in_dim(key_blocks, first_block, BLK_DEV, 0)
        own_values = lax.dynamic_slice_in_dim(value_blocks, first_block, BLK_DEV, 0)
        mixture = attend(own_queries, own_keys, own_values, far_keys, far_values, lists >= 0)
        return mixture.reshape(TOK_DEV, HEADS * HDIM).astype(jnp.bfloat16)
    attended = lax.map(one_shard, jnp.arange(N_CTX, dtype=jnp.int32)).reshape(SEQ, HEADS * HDIM)
    group_cols = HEADS * HDIM // N_HEAD

    def one_group(running, group):
        start_col = (group * group_cols).astype(jnp.int32)
        part_cols = lax.dynamic_slice_in_dim(attended, start_col, group_cols, 1)
        part_rows = lax.dynamic_slice_in_dim(w_out, start_col, group_cols, 0)
        term = jnp.dot(part_cols, part_rows, preferred_element_type=jnp.float32).astype(jnp.bfloat16)
        term = lax.optimization_barrier(term)
        return (running + term.astype(jnp.float32), None)
    summed, unused = lax.scan(one_group, jnp.zeros((SEQ, D), jnp.float32), jnp.arange(N_HEAD, dtype=jnp.int32))
    return summed.astype(jnp.bfloat16)
```

```python
import functools

import jax
import jax.numpy as jnp
import numpy as np
from jax import lax
from jax.experimental import pallas as pl
from jax.experimental.pallas import tpu as pltpu
from jax.sharding import PartitionSpec as P

D = 5120
HDIM = 128
BLOCK = 128
MAXA = 4
PER_GROUP = 5
QCOLS = PER_GROUP * HDIM
HALF = BLOCK // 2
ROPE_BASE = 1000000.0
Q_SCALE = float(HDIM**-0.5 * np.log2(np.e))
MESH = pl.DeviceIdType.MESH
F32 = jnp.float32
BF16 = jnp.bfloat16
N_OUT = 512


def rope_tables():
    frequency = ROPE_BASE ** (-2.0 * np.arange(HDIM // 2) / HDIM)
    frequency = np.concatenate([frequency, frequency])
    inner = np.arange(BLOCK)[:, None] * frequency[None, :]
    outer = np.arange(128)[:, None] * float(BLOCK) * frequency[None, :]
    return [f(t).astype(np.float32) for t in (inner, outer) for f in (np.cos, np.sin)]


def kernel(
    hid, gain, wq_h, wk_h, wv_h, wo_h, anc_h, ci, si, cb, sb,
    out,
    xb, wkv, wq, wo, qs, kv, att, rb, far, fin, anc_v, anc_s,
    ag_s, ag_r, ws_s, ws_r, wz_s, wl, kv_s, kv_r, rs_s, rs_r, an_s, an_r, an_l,
):
    c = lax.axis_index("ctx")
    h = lax.axis_index("head")
    x = h // 2
    par = h % 2
    yh = (c // 2) % 2
    z = c // 4
    k = c % 2
    y = yh * 2 + par
    zp = z % 2
    span = 2 * z + yh
    own = k == par

    def dev(x, y, z, k):
        return {"ctx": z * 4 + (y // 2) * 2 + k, "head": x * 2 + y % 2}

    right = dev((x + 1) % 4, y, z, k)
    left = dev((x + 3) % 4, y, z, k)
    sib = dev(x, y, z, 1 - k)

    def send(src, dst, ssem, rsem, to):
        return pltpu.make_async_remote_copy(
            src_ref=src, dst_ref=dst, send_sem=ssem, recv_sem=rsem, device_id=to, device_id_type=MESH
        )

    barrier = pltpu.get_barrier_semaphore()
    greeted = [right, left, sib]
    greeted += [dev(x, (y + d) % 4, z, k) for d in (1, 2, 3)]
    greeted += [dev(x, (y + d) % 4, z, 1 - k) for d in (1, 3)]
    greeted += [dev(x, (y + d) % 4, (z + e) % 4, k) for e in (1, 3) for d in range(4)]
    for to in greeted:
        pl.semaphore_signal(barrier, 1, device_id=to, device_id_type=MESH)

    local = [
        pltpu.make_async_copy(wk_h, wkv.at[:, pl.ds(0, HDIM)], wl.at[0]),
        pltpu.make_async_copy(wv_h, wkv.at[:, pl.ds(HDIM, HDIM)], wl.at[1]),
        pltpu.make_async_copy(wq_h, wq, wl.at[2]),
        pltpu.make_async_copy(wo_h, wo, wl.at[3]),
    ]

    @pl.when(own)
    def _():
        for copy in local:
            copy.start()

    anc_local = pltpu.make_async_copy(anc_h, anc_s.at[k], an_l.at[0])
    anc_local.start()

    def rows_of(core, first, count):
        return pl.ds(pl.multiple_of(core * BLOCK + first, HALF), count)

    @pl.loop(0, BLOCK // 16)
    def _(i):
        rows = pl.ds(pl.multiple_of(i * 16, 16), 16)
        v = hid[rows, :].astype(F32)
        scale = lax.rsqrt(jnp.mean(v * v, axis=1, keepdims=True) + 1e-06)
        xb[0, pl.ds(pl.multiple_of(k * BLOCK + i * 16, 16), 16), :] = (v * scale * gain[...]).astype(BF16)

    pl.semaphore_wait(barrier, len(greeted))

    A, B = (0, HALF), (HALF, HALF)
    routes = [
        (0, 1, A, right), (0, 1, B, right), (0, 3, B, left), (0, 3, A, left), (0, 0, (0, BLOCK), sib),
        (1, 2, A, right), (3, 2, B, left),
        (1, 1, A, sib), (1, 1, B, sib), (3, 3, B, sib), (3, 3, A, sib), (2, 2, A, sib), (2, 2, B, sib),
    ]

    def ag(m):
        s, t, (first, count), to = routes[m]
        rows = rows_of(k, first, count)
        return send(xb.at[s, rows, :], xb.at[t, rows, :], ag_s.at[m], ag_r.at[m], to)

    for m in range(5):
        ag(m).start()

    anc_send = send(anc_h, anc_v, an_s.at[0], an_r.at[0], sib)
    anc_send.start()

    def chunk(n, quarter):
        def rows(size, part, parts):
            return pl.ds(pl.multiple_of(quarter * size + part * (size // parts), 16), size // parts)

        if n == 0:
            r = rows(D // 4, 0, 1)
            return wk_h.at[r, :], wkv.at[r, pl.ds(0, HDIM)]
        if n == 1:
            r = rows(D // 4, 0, 1)
            return wv_h.at[r, :], wkv.at[r, pl.ds(HDIM, HDIM)]
        if n in (2, 3):
            r = rows(D // 4, n - 2, 2)
            return wq_h.at[r, :], wq.at[r, :]
        r = rows(QCOLS // 4, n - 4, 2)
        return wo_h.at[r, :], wo.at[r, :]

    y_target = dev(x, (y + 3 + 2 * k) % 4, z, par)

    def w_out_send(n):
        quarter = 2 * zp + k
        src, dst = chunk(n, quarter)
        return send(src, dst, ws_s.at[n], ws_r.at[n, quarter], y_target)

    def w_arrival(n, quarter):
        _, dst = chunk(n, quarter)
        return send(dst, dst, ws_s.at[n], ws_r.at[n, quarter], y_target)

    def w_pass(n, side):
        quarter = 2 * zp + side
        _, dst = chunk(n, quarter)
        to = dev(x, y, (z + 1 + 2 * side) % 4, k)
        return send(dst, dst, wz_s.at[n, side], ws_r.at[n, quarter], to)

    def pass_weights(chunks):
        @pl.when(jnp.logical_not(own))
        def _():
            for n in chunks:
                for side in range(2):
                    w_arrival(n, 2 * zp + side).wait_recv()
                    w_pass(n, side).start()

    def wait_weights(chunks, locals_):
        @pl.when(own)
        def _():
            for i in locals_:
                local[i].wait()

        @pl.when(jnp.logical_not(own))
        def _():
            for n in chunks:
                for side in range(2):
                    w_arrival(n, 2 * (1 - zp) + side).wait_recv()

    for n in range(4):
        w_out_send(n).start()

    pass_weights((0, 1))

    def rope(block):
        cos_b, sin_b = cb[pl.ds(block, 1), :], sb[pl.ds(block, 1), :]
        cosine = cos_b * ci[...] - sin_b * si[...]
        sine = sin_b * ci[...] + cos_b * si[...]
        lane = lax.broadcasted_iota(jnp.int32, (BLOCK, HDIM), 1)
        return cosine, jnp.where(lane < HDIM // 2, -sine, sine)

    def rotated(v, table):
        return v * table[0] + pltpu.roll(v, HDIM // 2, 1) * table[1]

    def x_of(r):
        return (x + 4 - r) % 4

    def block_of(r, core):
        return 16 * span + 8 * core + 2 * x_of(r) + par

    def project_kv(r):
        both = jnp.dot(xb[r], wkv[...], preferred_element_type=F32)
        for core in range(2):
            part = both[core * BLOCK : (core + 1) * BLOCK]
            slot = 48 + 8 * par + 2 * x_of(r) + core
            kv[slot, 0] = rotated(part[:, :HDIM], rope(block_of(r, core))).astype(BF16)
            kv[slot, 1] = part[:, HDIM:].astype(BF16)

    def project_q(r):
        for first, count in ((0, 2), (2, 2), (4, 1)):
            got = jnp.dot(xb[r], wq[:, first * HDIM : (first + count) * HDIM], preferred_element_type=F32)
            for core in range(2):
                table = rope(block_of(r, core))
                for e in range(count):
                    part = got[core * BLOCK : (core + 1) * BLOCK, e * HDIM : (e + 1) * HDIM]
                    qs[r, core, first + e] = (rotated(part, table) * Q_SCALE).astype(BF16)

    def kv_pair(region, r):
        return kv.at[pl.ds(16 * region + 8 * par + 2 * x_of(r), 2)]

    def kv_sem(region, parity, r):
        return kv_r.at[region * 8 + parity * 4 + r]

    partner = dev(x, yh * 2 + 1 - par, z, k)

    def other(t):
        return dev(x, (1 - yh) * 2 + t, z, k)

    def kv_up(r):
        return send(kv_pair(3, r), kv_pair(1, r), kv_s.at[r], kv_sem(1, par, r), dev(x, y, (z + 1) % 4, k))

    def kv_partner(r):
        return send(kv_pair(3, r), kv_pair(3, r), kv_s.at[4 + r], kv_sem(3, par, r), partner)

    def kv_next(r, t):
        return send(kv_pair(3, r), kv_pair(2, r), kv_s.at[8 + 2 * r + t], kv_sem(2, par, r), other(t))

    def kv_pass_partner(r):
        return send(kv_pair(1, r), kv_pair(1, r), kv_s.at[16 + r], kv_sem(1, par, r), partner)

    def kv_pass_next(r, t):
        return send(kv_pair(1, r), kv_pair(2, r), kv_s.at[20 + 2 * r + t], kv_sem(2, par, r), other(t))

    def kv_far(i, t):
        slot = 8 * par + 5 + 2 * i
        to = dev(x, (1 - yh) * 2 + t, (z + yh) % 4, k)
        return send(kv.at[pl.ds(16 + slot, 1)], kv.at[pl.ds(slot, 1)], kv_s.at[28 + 2 * i + t], kv_sem(0, par, i), to)

    far_sends = jnp.logical_and(z > 0, z + yh < 4)

    def start_kv(r):
        @pl.when(z < 3)
        def _():
            kv_up(r).start()

        kv_partner(r).start()

        @pl.when(yh == 0)
        def _():
            for t in range(2):
                kv_next(r, t).start()

    def pass_kv(r):
        @pl.when(z > 0)
        def _():
            kv_up(r).wait_recv()
            kv_pass_partner(r).start()

            @pl.when(yh == 1)
            def _():
                for t in range(2):
                    kv_pass_next(r, t).start()

    ag(0).wait_recv()
    ag(5).start()
    ag(7).start()
    ag(2).wait_recv()
    ag(6).start()
    ag(9).start()
    pass_weights((2, 3))
    wait_weights((0, 1), (0, 1))
    ag(4).wait_recv()
    project_kv(0)
    ag(1).wait_recv()
    ag(8).start()
    ag(3).wait_recv()
    ag(10).start()
    for m in (7, 8, 9, 10):
        ag(m).wait_recv()

    @pl.loop(0, 2)
    def _(i):
        project_kv(1 + 2 * i)

    for r in (0, 1, 3):
        start_kv(r)
    for n in (4, 5):
        w_out_send(n).start()
    wait_weights((2, 3), (2,))

    @pl.loop(0, 3)
    def _(i):
        project_q(i + i // 2)

    for r in (0, 1, 3):
        pass_kv(r)
    for m in (5, 6):
        ag(m).wait_recv()
        ag(m + 6).start()
    for m in (11, 12):
        ag(m).wait_recv()
    project_kv(2)
    start_kv(2)
    project_q(2)
    pass_kv(2)

    @pl.when(far_sends)
    def _():
        for i in range(2):
            for t in range(2):
                kv_far(i, t).start()

    pass_weights((4, 5))
    for m in range(13):
        ag(m).wait_send()

    anc_local.wait()
    anc_send.wait()
    anc_move = pltpu.make_async_copy(anc_v, anc_s.at[1 - k], an_l.at[1])
    anc_move.start()
    anc_move.wait()

    def kv_arrival(region, parity, r, blocks):
        ref = kv.at[pl.ds(16 * region + 8 * parity + 2 * r, blocks)]
        return send(ref, ref, kv_s.at[0], kv_sem(region, parity, r), partner)

    for r in range(4):
        kv_arrival(3, 1 - par, r, 2).wait_recv()

    @pl.when(span >= 1)
    def _():
        for parity in range(2):
            for r in range(4):
                kv_arrival(2, parity, r, 2).wait_recv()

    @pl.when(span >= 2)
    def _():
        for r in range(4):
            kv_arrival(1, 1 - par, r, 2).wait_recv()

    @pl.when(span >= 3)
    def _():
        for parity in range(2):
            for i in range(2):
                kv_arrival(0, parity, i, 1).wait_recv()

    def attend(r):
        xr = x_of(r)

        @pl.loop(0, 2)
        def _(core):
            row = 2 * xr + par
            mine = 48 + 8 * par + 2 * xr + core
            keys, values, biases = [kv[mine, 0]], [kv[mine, 1]], [None]
            for j in range(MAXA):
                a = anc_s[core, row, j]
                listed = a >= 0
                place = jnp.where(listed, jnp.clip(a - 16 * span + 48, 0, 63), 48 + 8 * core + row)
                within = place % 16
                slot = (place // 16) * 16 + (within % 2) * 8 + ((within // 2) % 4) * 2 + within // 8
                keys.append(kv[slot, 0])
                values.append(kv[slot, 1])
                biases.append(jnp.where(listed, 0.0, -1e30).astype(F32))
            causal = lax.broadcasted_iota(jnp.int32, (BLOCK, BLOCK), 0) >= lax.broadcasted_iota(
                jnp.int32, (BLOCK, BLOCK), 1
            )
            for e in range(PER_GROUP):
                q = qs[r, core, e]
                scores = []
                for key, bias in zip(keys, biases):
                    s = lax.dot_general(q, key, (((1,), (1,)), ((), ())), preferred_element_type=F32)
                    scores.append(jnp.where(causal, s, -1e30) if bias is None else s + bias)
                top = functools.reduce(jnp.maximum, scores).max(axis=1, keepdims=True)
                weights = [jnp.exp2(s - top) for s in scores]
                total = functools.reduce(jnp.add, weights).sum(axis=1, keepdims=True)
                mixture = sum(
                    jnp.dot(w.astype(BF16), v, preferred_element_type=F32) for w, v in zip(weights, values)
                )
                att[rows_of(core, 0, BLOCK), e * HDIM : (e + 1) * HDIM] = (mixture / total).astype(BF16)

    def project_out(r):
        @pl.loop(0, D // N_OUT)
        def _(n):
            cols = pl.ds(pl.multiple_of(n * N_OUT, N_OUT), N_OUT)
            xb[r, :, cols] = jnp.dot(att[...], wo[:, cols], preferred_element_type=F32).astype(BF16)

    def to_sibling(r):
        return send(xb.at[r, rows_of(1 - k, 0, BLOCK), :], rb.at[r], rs_s.at[r], rs_r.at[r], sib)

    def add_into(r, first, count, terms):
        @pl.loop(0, count // 16)
        def _(i):
            at = pl.multiple_of(first + i * 16, 16)
            rows = pl.ds(pl.multiple_of(k * BLOCK + first + i * 16, 16), 16)
            total = xb[r, rows, :].astype(F32)
            for term in terms:
                total = total + term(at).astype(F32)
            xb[r, rows, :] = total.astype(BF16)

    def half(r, first):
        return xb.at[r, rows_of(k, first, HALF), :]

    def far_send(side):
        return send(half(2, side * HALF), far.at[side], rs_s.at[4 + side], rs_r.at[4 + side], (right, left)[side])

    def fin_send(side, first):
        n = 6 + 2 * side + first // HALF
        dst = fin.at[side, pl.ds(first, HALF), :]
        return send(half((3, 1)[side], first), dst, rs_s.at[n], rs_r.at[n], (right, left)[side])

    def take_sibling(r):
        to_sibling(r).wait_recv()
        add_into(r, 0, BLOCK, [lambda at: rb[r, pl.ds(at, 16), :]])

    attend(2)
    wait_weights((4, 5), (3,))
    project_out(2)
    to_sibling(2).start()
    attend(3)
    take_sibling(2)
    for side in range(2):
        far_send(side).start()
    project_out(3)
    to_sibling(3).start()
    attend(1)
    project_out(1)
    to_sibling(1).start()
    take_sibling(3)
    fin_send(0, HALF).start()
    take_sibling(1)
    fin_send(1, 0).start()
    attend(0)
    project_out(0)
    to_sibling(0).start()
    for side, r, first in ((0, 3, 0), (1, 1, HALF)):
        far_send(side).wait_recv()
        add_into(r, first, HALF, [lambda at: far[side, pl.ds(at - first, 16), :]])
        fin_send(side, first).start()
    to_sibling(0).wait_recv()
    for n, (side, first) in enumerate(((0, HALF), (1, 0), (0, 0), (1, HALF))):
        fin_send(side, first).wait_recv()

    @pl.loop(0, BLOCK // 16)
    def _(i):
        at = pl.ds(pl.multiple_of(i * 16, 16), 16)
        rows = pl.ds(pl.multiple_of(k * BLOCK + i * 16, 16), 16)
        total = xb[0, rows, :].astype(F32) + rb[0, at, :].astype(F32)
        total = total + fin[0, at, :].astype(F32) + fin[1, at, :].astype(F32)
        out[at, :] = total.astype(BF16)

    for r in range(4):
        to_sibling(r).wait_send()
        kv_partner(r).wait_send()
    for side in range(2):
        far_send(side).wait_send()
        for first in (0, HALF):
            fin_send(side, first).wait_send()
    for n in range(6):
        w_out_send(n).wait_send()

    @pl.when(jnp.logical_not(own))
    def _():
        for n in range(6):
            for side in range(2):
                w_pass(n, side).wait_send()

    @pl.when(z < 3)
    def _():
        for r in range(4):
            kv_up(r).wait_send()

    @pl.when(yh == 0)
    def _():
        for r in range(4):
            for t in range(2):
                kv_next(r, t).wait_send()

    @pl.when(z > 0)
    def _():
        for r in range(4):
            kv_pass_partner(r).wait_send()

    @pl.when(jnp.logical_and(z > 0, yh == 1))
    def _():
        for r in range(4):
            for t in range(2):
                kv_pass_next(r, t).wait_send()

    @pl.when(far_sends)
    def _():
        for i in range(2):
            for t in range(2):
                kv_far(i, t).wait_send()


def on_device(hidden_rows, norm_gain, w_query, w_key, w_value, w_out, ancestors):
    vmem = pl.BlockSpec(memory_space=pltpu.VMEM)
    hbm = pl.BlockSpec(memory_space=pl.ANY)
    dma = pltpu.SemaphoreType.DMA
    lists = jnp.pad(ancestors, ((0, 0), (0, 128 - MAXA)))
    return pl.pallas_call(
        kernel,
        out_shape=jax.ShapeDtypeStruct((BLOCK, D), BF16),
        in_specs=[vmem, vmem, hbm, hbm, hbm, hbm, hbm, vmem, vmem, vmem, vmem],
        out_specs=vmem,
        scratch_shapes=[
            pltpu.VMEM((4, 2 * BLOCK, D), BF16),
            pltpu.VMEM((D, 2 * HDIM), BF16),
            pltpu.VMEM((D, QCOLS), BF16),
            pltpu.VMEM((QCOLS, D), BF16),
            pltpu.VMEM((4, 2, PER_GROUP, BLOCK, HDIM), BF16),
            pltpu.VMEM((64, 2, BLOCK, HDIM), BF16),
            pltpu.VMEM((2 * BLOCK, QCOLS), BF16),
            pltpu.VMEM((4, BLOCK, D), BF16),
            pltpu.VMEM((2, HALF, D), BF16),
            pltpu.VMEM((2, BLOCK, D), BF16),
            pltpu.VMEM((8, 128), jnp.int32),
            pltpu.SMEM((2, 8, 128), jnp.int32),
            dma((13,)),
            dma((13,)),
            dma((6,)),
            dma((6, 4)),
            dma((6, 2)),
            dma((4,)),
            dma((32,)),
            dma((32,)),
            dma((10,)),
            dma((10,)),
            dma((1,)),
            dma((1,)),
            dma((2,)),
        ],
        compiler_params=pltpu.CompilerParams(
            collective_id=0, has_side_effects=True, vmem_limit_bytes=60 * 2**20
        ),
        cost_estimate=pl.CostEstimate(
            flops=17 * 10**9, bytes_accessed=20 * 10**6, transcendentals=4 * 10**6
        ),
    )(
        hidden_rows, norm_gain.reshape(1, D), w_query, w_key, w_value, w_out, lists,
        *[jnp.asarray(t) for t in rope_tables()],
    )


def solution(mesh):
    placed = (
        P(("ctx", "head"), None),
        P(),
        P(None, "head"),
        P(None, "head"),
        P(None, "head"),
        P("head", None),
        P("ctx", None),
    )
    return jax.shard_map(
        on_device, mesh=mesh, in_specs=placed, out_specs=P(("ctx", "head"), None), check_vma=False
    )
```

```python
import functools

import jax
import jax.numpy as jnp
import numpy as np
from jax import lax
from jax.experimental import pallas as pl
from jax.experimental.pallas import tpu as pltpu
from jax.sharding import PartitionSpec as P

D = 5120
HDIM = 128
BLOCK = 128
MAXA = 4
PER_GROUP = 5
QCOLS = PER_GROUP * HDIM
HALF = BLOCK // 2
ROPE_BASE = 1000000.0
Q_SCALE = float(HDIM**-0.5 * np.log2(np.e))
MESH = pl.DeviceIdType.MESH
F32 = jnp.float32
BF16 = jnp.bfloat16
N_OUT = 512
WIDE = D // 2


def rope_tables():
    frequency = ROPE_BASE ** (-2.0 * np.arange(HDIM // 2) / HDIM)
    frequency = np.concatenate([frequency, frequency])
    inner = np.arange(BLOCK)[:, None] * frequency[None, :]
    outer = np.arange(128)[:, None] * float(BLOCK) * frequency[None, :]
    return [f(t).astype(np.float32) for t in (inner, outer) for f in (np.cos, np.sin)]


def kernel(
    hid, gain, wq_h, wk_h, wv_h, wo_h, anc_h, ci, si, cb, sb,
    out,
    xb, wkv, wq, wo, qs, kv, att, rb, far, fin, anc_v, anc_s,
    ag_s, ag_r, ws_s, ws_r, wz_s, wl, kv_s, kv_r, rs_s, rs_r, an_s, an_r, an_l,
):
    c = lax.axis_index("ctx")
    h = lax.axis_index("head")
    x = h // 2
    par = h % 2
    yh = (c // 2) % 2
    z = c // 4
    k = c % 2
    y = yh * 2 + par
    zp = z % 2
    span = 2 * z + yh
    own = k == par

    def dev(x, y, z, k):
        return {"ctx": z * 4 + (y // 2) * 2 + k, "head": x * 2 + y % 2}

    right = dev((x + 1) % 4, y, z, k)
    left = dev((x + 3) % 4, y, z, k)
    sib = dev(x, y, z, 1 - k)

    def send(src, dst, ssem, rsem, to):
        return pltpu.make_async_remote_copy(
            src_ref=src, dst_ref=dst, send_sem=ssem, recv_sem=rsem, device_id=to, device_id_type=MESH
        )

    barrier = pltpu.get_barrier_semaphore()
    partner = dev(x, yh * 2 + 1 - par, z, k)
    cross_y = (1 - yh) * 2 + 1 - par
    cross = dev(x, cross_y, z, k)
    above = dev(x, y, (z + 1) % 4, k)
    greeted = [right, left, sib, partner, cross, above, dev(x, y, (z + 3) % 4, k)]
    greeted += [dev(x, (y + d) % 4, z, 1 - k) for d in (1, 3)]
    greeted += [dev(x, cross_y, (z + 3 + 2 * yh) % 4, k)]
    for to in greeted:
        pl.semaphore_signal(barrier, 1, device_id=to, device_id_type=MESH)

    local = [
        pltpu.make_async_copy(wk_h, wkv.at[:, pl.ds(0, HDIM)], wl.at[0]),
        pltpu.make_async_copy(wv_h, wkv.at[:, pl.ds(HDIM, HDIM)], wl.at[1]),
        pltpu.make_async_copy(wq_h, wq, wl.at[2]),
        pltpu.make_async_copy(wo_h, wo, wl.at[3]),
    ]

    @pl.when(own)
    def _():
        for copy in local:
            copy.start()

    anc_local = pltpu.make_async_copy(anc_h, anc_s.at[k], an_l.at[0])
    anc_local.start()

    def rows_of(core, first, count):
        return pl.ds(pl.multiple_of(core * BLOCK + first, HALF), count)

    @pl.loop(0, BLOCK // 16)
    def _(i):
        rows = pl.ds(pl.multiple_of(i * 16, 16), 16)
        v = hid[rows, :].astype(F32)
        scale = lax.rsqrt(jnp.mean(v * v, axis=1, keepdims=True) + 1e-06)
        xb[0, pl.ds(pl.multiple_of(k * BLOCK + i * 16, 16), 16), :] = (v * scale * gain[...]).astype(BF16)

    pl.semaphore_wait(barrier, len(greeted))

    A, B = (0, HALF), (HALF, HALF)
    routes = [
        (0, 1, A, right), (0, 1, B, right), (0, 3, B, left), (0, 3, A, left), (0, 0, (0, BLOCK), sib),
        (1, 2, A, right), (3, 2, B, left),
        (1, 1, A, sib), (1, 1, B, sib), (3, 3, B, sib), (3, 3, A, sib), (2, 2, A, sib), (2, 2, B, sib),
    ]

    def ag(m):
        s, t, (first, count), to = routes[m]
        rows = rows_of(k, first, count)
        return send(xb.at[s, rows, :], xb.at[t, rows, :], ag_s.at[m], ag_r.at[m], to)

    for m in range(5):
        ag(m).start()

    anc_send = send(anc_h, anc_v, an_s.at[0], an_r.at[0], sib)
    anc_send.start()

    def chunk(n, quarter):
        def rows(size, part, parts):
            return pl.ds(pl.multiple_of(quarter * size + part * (size // parts), 16), size // parts)

        if n == 0:
            r = rows(D // 4, 0, 1)
            return wk_h.at[r, :], wkv.at[r, pl.ds(0, HDIM)]
        if n == 1:
            r = rows(D // 4, 0, 1)
            return wv_h.at[r, :], wkv.at[r, pl.ds(HDIM, HDIM)]
        if n in (2, 3):
            r = rows(D // 4, n - 2, 2)
            return wq_h.at[r, :], wq.at[r, :]
        r = rows(QCOLS // 4, 0, 1)
        cols = pl.ds((n - 4) * WIDE, WIDE)
        return wo_h.at[r, cols], wo.at[r, cols]

    y_target = dev(x, (y + 3 + 2 * k) % 4, z, par)

    def w_out_send(n):
        quarter = 2 * zp + k
        src, dst = chunk(n, quarter)
        return send(src, dst, ws_s.at[n], ws_r.at[n, quarter], y_target)

    def w_arrival(n, quarter):
        _, dst = chunk(n, quarter)
        return send(dst, dst, ws_s.at[n], ws_r.at[n, quarter], y_target)

    def w_pass(n, side):
        quarter = 2 * zp + side
        _, dst = chunk(n, quarter)
        to = dev(x, y, (z + 1 + 2 * side) % 4, k)
        return send(dst, dst, wz_s.at[n, side], ws_r.at[n, quarter], to)

    def pass_weights(chunks):
        @pl.when(jnp.logical_not(own))
        def _():
            for n in chunks:
                for side in range(2):
                    w_arrival(n, 2 * zp + side).wait_recv()
                    w_pass(n, side).start()

    def wait_weights(chunks, locals_):
        @pl.when(own)
        def _():
            for i in locals_:
                local[i].wait()

        @pl.when(jnp.logical_not(own))
        def _():
            for n in chunks:
                for side in range(2):
                    w_arrival(n, 2 * (1 - zp) + side).wait_recv()

    for n in range(5):
        w_out_send(n).start()

    pass_weights((0, 1))

    def rope(block):
        cos_b, sin_b = cb[pl.ds(block, 1), :], sb[pl.ds(block, 1), :]
        cosine = cos_b * ci[...] - sin_b * si[...]
        sine = sin_b * ci[...] + cos_b * si[...]
        lane = lax.broadcasted_iota(jnp.int32, (BLOCK, HDIM), 1)
        return cosine, jnp.where(lane < HDIM // 2, -sine, sine)

    def rotated(v, table):
        return v * table[0] + pltpu.roll(v, HDIM // 2, 1) * table[1]

    def x_of(r):
        return (x + 4 - r) % 4

    def block_of(r, core):
        return 16 * span + 8 * core + 2 * x_of(r) + par

    def project_kv(r):
        both = jnp.dot(xb[r], wkv[...], preferred_element_type=F32)
        for core in range(2):
            part = both[core * BLOCK : (core + 1) * BLOCK]
            slot = 48 + 8 * par + 2 * x_of(r) + core
            kv[slot, 0] = rotated(part[:, :HDIM], rope(block_of(r, core))).astype(BF16)
            kv[slot, 1] = part[:, HDIM:].astype(BF16)

    def project_q(r):
        for first, count in ((0, 2), (2, 2), (4, 1)):
            got = jnp.dot(xb[r], wq[:, first * HDIM : (first + count) * HDIM], preferred_element_type=F32)
            for core in range(2):
                table = rope(block_of(r, core))
                for e in range(count):
                    part = got[core * BLOCK : (core + 1) * BLOCK, e * HDIM : (e + 1) * HDIM]
                    qs[r, core, first + e] = (rotated(part, table) * Q_SCALE).astype(BF16)

    def kv_pair(region, parity, r):
        return kv.at[pl.ds(16 * region + 8 * parity + 2 * x_of(r), 2)]

    def kv_send(n, src, dst, parity, r, to):
        return send(
            kv_pair(src, parity, r), kv_pair(dst, parity, r), kv_s.at[n], kv_r.at[dst * 8 + parity * 4 + r], to
        )

    def kv_up(r):
        return kv_send(r, 3, 1, par, r, above)

    def kv_partner(r, region):
        return kv_send((16 if region == 1 else 4) + r, region, region, par, r, partner)

    def kv_cross(r, region, mine):
        parity = par if mine else 1 - par
        return kv_send((20 if region == 1 else 8) + 2 * r + mine, region, 2, parity, r, cross)

    def kv_from_partner(r, region):
        return kv_send(0, region, region, 1 - par, r, partner)

    def kv_far(i, mine):
        parity = par if mine else 1 - par
        slot = 8 * parity + 5 + 2 * i
        to = dev(x, cross_y, (z + yh) % 4, k)
        return send(
            kv.at[pl.ds(16 + slot, 1)], kv.at[pl.ds(slot, 1)],
            kv_s.at[28 + 2 * i + mine], kv_r.at[parity * 4 + i], to,
        )

    far_sends = jnp.logical_and(z > 0, z + yh < 4)

    def start_kv(r):
        @pl.when(z < 3)
        def _():
            kv_up(r).start()

        kv_partner(r, 3).start()

        @pl.when(yh == 0)
        def _():
            kv_cross(r, 3, 1).start()

    def pass_kv(r):
        @pl.when(z > 0)
        def _():
            kv_up(r).wait_recv()
            kv_partner(r, 1).start()

            @pl.when(yh == 1)
            def _():
                kv_cross(r, 1, 1).start()

    def pass_partner_kv(r):
        kv_from_partner(r, 3).wait_recv()

        @pl.when(yh == 0)
        def _():
            kv_cross(r, 3, 0).start()

        @pl.when(z > 0)
        def _():
            kv_from_partner(r, 1).wait_recv()

            @pl.when(yh == 1)
            def _():
                kv_cross(r, 1, 0).start()

    ag(0).wait_recv()
    ag(5).start()
    ag(7).start()
    ag(2).wait_recv()
    ag(6).start()
    ag(9).start()
    pass_weights((2, 3))
    wait_weights((0, 1), (0, 1))
    ag(4).wait_recv()
    project_kv(0)
    ag(1).wait_recv()
    ag(8).start()
    ag(3).wait_recv()
    ag(10).start()
    for m in (7, 8, 9, 10):
        ag(m).wait_recv()

    @pl.loop(0, 2)
    def _(i):
        project_kv(1 + 2 * i)

    for r in (0, 1, 3):
        start_kv(r)
    w_out_send(5).start()
    pass_weights((4,))
    wait_weights((2, 3), (2,))

    @pl.loop(0, 3)
    def _(i):
        project_q(i + i // 2)

    for r in (0, 1, 3):
        pass_kv(r)
    for r in (0, 1, 3):
        pass_partner_kv(r)
    for m in (5, 6):
        ag(m).wait_recv()
        ag(m + 6).start()
    for m in (11, 12):
        ag(m).wait_recv()
    project_kv(2)
    start_kv(2)
    project_q(2)
    pass_kv(2)
    pass_partner_kv(2)

    @pl.when(far_sends)
    def _():
        for i in range(2):
            for mine in range(2):
                kv_far(i, mine).start()

    for m in range(13):
        ag(m).wait_send()

    anc_local.wait()
    anc_send.wait()
    anc_move = pltpu.make_async_copy(anc_v, anc_s.at[1 - k], an_l.at[1])
    anc_move.start()
    anc_move.wait()

    def kv_arrival(region, parity, r, blocks):
        ref = kv.at[pl.ds(16 * region + 8 * parity + 2 * r, blocks)]
        return send(ref, ref, kv_s.at[0], kv_r.at[region * 8 + parity * 4 + r], partner)

    @pl.when(span >= 1)
    def _():
        for parity in range(2):
            for r in range(4):
                kv_arrival(2, parity, r, 2).wait_recv()

    @pl.when(span >= 3)
    def _():
        for parity in range(2):
            for i in range(2):
                kv_arrival(0, parity, i, 1).wait_recv()

    def attend(r):
        xr = x_of(r)

        @pl.loop(0, 2)
        def _(core):
            row = 2 * xr + par
            mine = 48 + 8 * par + 2 * xr + core
            keys, values, biases = [kv[mine, 0]], [kv[mine, 1]], [None]
            for j in range(MAXA):
                a = anc_s[core, row, j]
                listed = a >= 0
                place = jnp.where(listed, jnp.clip(a - 16 * span + 48, 0, 63), 48 + 8 * core + row)
                within = place % 16
                slot = (place // 16) * 16 + (within % 2) * 8 + ((within // 2) % 4) * 2 + within // 8
                keys.append(kv[slot, 0])
                values.append(kv[slot, 1])
                biases.append(jnp.where(listed, 0.0, -1e30).astype(F32))
            causal = lax.broadcasted_iota(jnp.int32, (BLOCK, BLOCK), 0) >= lax.broadcasted_iota(
                jnp.int32, (BLOCK, BLOCK), 1
            )
            for e in range(PER_GROUP):
                q = qs[r, core, e]
                scores = []
                for key, bias in zip(keys, biases):
                    s = lax.dot_general(q, key, (((1,), (1,)), ((), ())), preferred_element_type=F32)
                    scores.append(jnp.where(causal, s, -1e30) if bias is None else s + bias)
                top = functools.reduce(jnp.maximum, scores).max(axis=1, keepdims=True)
                weights = [jnp.exp2(s - top) for s in scores]
                total = functools.reduce(jnp.add, weights).sum(axis=1, keepdims=True)
                mixture = sum(
                    jnp.dot(w.astype(BF16), v, preferred_element_type=F32) for w, v in zip(weights, values)
                )
                att[r, rows_of(core, 0, BLOCK), e * HDIM : (e + 1) * HDIM] = (mixture / total).astype(BF16)

    def wide(j):
        return pl.ds(j * WIDE, WIDE)

    def project_out(r, j):
        @pl.loop(0, WIDE // N_OUT)
        def _(n):
            cols = pl.ds(pl.multiple_of(j * WIDE + n * N_OUT, N_OUT), N_OUT)
            xb[r, :, cols] = jnp.dot(att[r], wo[:, cols], preferred_element_type=F32).astype(BF16)

    def to_sibling(r, j):
        n = 4 * j + r
        src = xb.at[r, rows_of(1 - k, 0, BLOCK), wide(j)]
        return send(src, rb.at[r, :, wide(j)], rs_s.at[n], rs_r.at[n], sib)

    def add_into(r, j, first, count, term):
        @pl.loop(0, count // 16)
        def _(i):
            at = pl.ds(pl.multiple_of(i * 16, 16), 16)
            rows = pl.ds(pl.multiple_of(k * BLOCK + first + i * 16, 16), 16)
            total = xb[r, rows, wide(j)].astype(F32) + term[at, wide(j)].astype(F32)
            xb[r, rows, wide(j)] = total.astype(BF16)

    def half(r, j, first):
        return xb.at[r, rows_of(k, first, HALF), wide(j)]

    def far_send(side, j):
        n = 8 + 2 * j + side
        return send(half(2, j, side * HALF), far.at[side, :, wide(j)], rs_s.at[n], rs_r.at[n], (right, left)[side])

    def fin_send(side, j, first):
        n = 12 + 4 * j + 2 * side + first // HALF
        dst = fin.at[side, pl.ds(first, HALF), wide(j)]
        return send(half((3, 1)[side], j, first), dst, rs_s.at[n], rs_r.at[n], (right, left)[side])

    def take_sibling(r, j):
        to_sibling(r, j).wait_recv()
        add_into(r, j, 0, BLOCK, rb.at[r])

    def put_out(r, j):
        project_out(r, j)
        to_sibling(r, j).start()

    def open_half(j, attend):
        put_out(2, j)
        attend(3)
        take_sibling(2, j)
        for side in range(2):
            far_send(side, j).start()
        put_out(3, j)
        attend(1)
        put_out(1, j)
        take_sibling(3, j)
        fin_send(0, j, HALF).start()
        take_sibling(1, j)
        fin_send(1, j, 0).start()
        attend(0)
        put_out(0, j)

    def close_half(j):
        for side, r, first in ((0, 3, 0), (1, 1, HALF)):
            far_send(side, j).wait_recv()
            add_into(r, j, first, HALF, far.at[side])
            fin_send(side, j, first).start()

    def finish(j):
        to_sibling(0, j).wait_recv()
        for side, first in ((0, HALF), (1, 0), (0, 0), (1, HALF)):
            fin_send(side, j, first).wait_recv()

        @pl.loop(0, BLOCK // 16)
        def _(i):
            at = pl.ds(pl.multiple_of(i * 16, 16), 16)
            rows = pl.ds(pl.multiple_of(k * BLOCK + i * 16, 16), 16)
            total = xb[0, rows, wide(j)].astype(F32) + rb[0, at, wide(j)].astype(F32)
            total = total + fin[0, at, wide(j)].astype(F32) + fin[1, at, wide(j)].astype(F32)
            out[at, wide(j)] = total.astype(BF16)

    attend(2)
    wait_weights((4,), (3,))
    open_half(0, attend)
    pass_weights((5,))
    close_half(0)
    wait_weights((5,), ())
    open_half(1, lambda r: None)
    finish(0)
    close_half(1)
    finish(1)

    for r in range(4):
        for j in range(2):
            to_sibling(r, j).wait_send()
        kv_partner(r, 3).wait_send()
    for j in range(2):
        for side in range(2):
            far_send(side, j).wait_send()
            for first in (0, HALF):
                fin_send(side, j, first).wait_send()
    for n in range(6):
        w_out_send(n).wait_send()

    @pl.when(jnp.logical_not(own))
    def _():
        for n in range(6):
            for side in range(2):
                w_pass(n, side).wait_send()

    @pl.when(z < 3)
    def _():
        for r in range(4):
            kv_up(r).wait_send()

    @pl.when(yh == 0)
    def _():
        for r in range(4):
            for mine in range(2):
                kv_cross(r, 3, mine).wait_send()

    @pl.when(z > 0)
    def _():
        for r in range(4):
            kv_partner(r, 1).wait_send()

    @pl.when(jnp.logical_and(z > 0, yh == 1))
    def _():
        for r in range(4):
            for mine in range(2):
                kv_cross(r, 1, mine).wait_send()

    @pl.when(far_sends)
    def _():
        for i in range(2):
            for mine in range(2):
                kv_far(i, mine).wait_send()


def on_device(hidden_rows, norm_gain, w_query, w_key, w_value, w_out, ancestors):
    vmem = pl.BlockSpec(memory_space=pltpu.VMEM)
    hbm = pl.BlockSpec(memory_space=pl.ANY)
    dma = pltpu.SemaphoreType.DMA
    lists = jnp.pad(ancestors, ((0, 0), (0, 128 - MAXA)))
    return pl.pallas_call(
        kernel,
        out_shape=jax.ShapeDtypeStruct((BLOCK, D), BF16),
        in_specs=[vmem, vmem, hbm, hbm, hbm, hbm, hbm, vmem, vmem, vmem, vmem],
        out_specs=vmem,
        scratch_shapes=[
            pltpu.VMEM((4, 2 * BLOCK, D), BF16),
            pltpu.VMEM((D, 2 * HDIM), BF16),
            pltpu.VMEM((D, QCOLS), BF16),
            pltpu.VMEM((QCOLS, D), BF16),
            pltpu.VMEM((4, 2, PER_GROUP, BLOCK, HDIM), BF16),
            pltpu.VMEM((64, 2, BLOCK, HDIM), BF16),
            pltpu.VMEM((4, 2 * BLOCK, QCOLS), BF16),
            pltpu.VMEM((4, BLOCK, D), BF16),
            pltpu.VMEM((2, HALF, D), BF16),
            pltpu.VMEM((2, BLOCK, D), BF16),
            pltpu.VMEM((8, 128), jnp.int32),
            pltpu.SMEM((2, 8, 128), jnp.int32),
            dma((13,)),
            dma((13,)),
            dma((6,)),
            dma((6, 4)),
            dma((6, 2)),
            dma((4,)),
            dma((32,)),
            dma((32,)),
            dma((20,)),
            dma((20,)),
            dma((1,)),
            dma((1,)),
            dma((2,)),
        ],
        compiler_params=pltpu.CompilerParams(
            collective_id=0, has_side_effects=True, vmem_limit_bytes=60 * 2**20
        ),
        cost_estimate=pl.CostEstimate(
            flops=17 * 10**9, bytes_accessed=20 * 10**6, transcendentals=4 * 10**6
        ),
    )(
        hidden_rows, norm_gain.reshape(1, D), w_query, w_key, w_value, w_out, lists,
        *[jnp.asarray(t) for t in rope_tables()],
    )


def solution(mesh):
    placed = (
        P(("ctx", "head"), None),
        P(),
        P(None, "head"),
        P(None, "head"),
        P(None, "head"),
        P("head", None),
        P("ctx", None),
    )
    return jax.shard_map(
        on_device, mesh=mesh, in_specs=placed, out_specs=P(("ctx", "head"), None), check_vma=False
    )
```

```python
import functools

import jax
import jax.numpy as jnp
import numpy as np
from jax import lax
from jax.experimental import pallas as pl
from jax.experimental.pallas import tpu as pltpu
from jax.sharding import PartitionSpec as P

D = 5120
HDIM = 128
BLOCK = 128
MAXA = 4
PER_GROUP = 5
QCOLS = PER_GROUP * HDIM
HALF = BLOCK // 2
ROPE_BASE = 1000000.0
Q_SCALE = float(HDIM**-0.5 * np.log2(np.e))
MESH = pl.DeviceIdType.MESH
F32 = jnp.float32
BF16 = jnp.bfloat16
N_OUT = 512
WIDE = D // 2


def rope_tables():
    frequency = ROPE_BASE ** (-2.0 * np.arange(HDIM // 2) / HDIM)
    frequency = np.concatenate([frequency, frequency])
    inner = np.arange(BLOCK)[:, None] * frequency[None, :]
    outer = np.arange(128)[:, None] * float(BLOCK) * frequency[None, :]
    return [f(t).astype(np.float32) for t in (inner, outer) for f in (np.cos, np.sin)]


def kernel(
    hid, gain, wq_h, wk_h, wv_h, wo_h, anc_h, ci, si, cb, sb,
    out,
    xb, wkv, wq, wo, qs, kv, att, rb, far, fin, anc_v, anc_s,
    ag_s, ag_r, ws_s, ws_r, wz_s, wl, kv_s, kv_r, rs_s, rs_r, an_s, an_r, an_l,
):
    c = lax.axis_index("ctx")
    h = lax.axis_index("head")
    x = h // 2
    par = h % 2
    yh = (c // 2) % 2
    z = c // 4
    k = c % 2
    y = yh * 2 + par
    zp = z % 2
    span = 2 * z + yh
    own = k == par

    def dev(x, y, z, k):
        return {"ctx": z * 4 + (y // 2) * 2 + k, "head": x * 2 + y % 2}

    right = dev((x + 1) % 4, y, z, k)
    left = dev((x + 3) % 4, y, z, k)
    sib = dev(x, y, z, 1 - k)

    def send(src, dst, ssem, rsem, to):
        return pltpu.make_async_remote_copy(
            src_ref=src, dst_ref=dst, send_sem=ssem, recv_sem=rsem, device_id=to, device_id_type=MESH
        )

    barrier = pltpu.get_barrier_semaphore()
    partner = dev(x, yh * 2 + 1 - par, z, k)
    cross_y = (1 - yh) * 2 + 1 - par
    cross = dev(x, cross_y, z, k)
    above = dev(x, y, (z + 1) % 4, k)
    greeted = [right, left, sib, partner, cross, above, dev(x, y, (z + 3) % 4, k)]
    greeted += [dev(x, (y + d) % 4, z, 1 - k) for d in (1, 3)]
    opposite_y = (1 - yh) * 2 + par
    opposite = dev(x, opposite_y, z, k)
    next_z = (z + 3 + 2 * yh) % 4
    greeted += [opposite, dev(x, cross_y, next_z, k), dev(x, opposite_y, next_z, k)]
    for to in greeted:
        pl.semaphore_signal(barrier, 1, device_id=to, device_id_type=MESH)

    local = [
        pltpu.make_async_copy(wk_h, wkv.at[:, pl.ds(0, HDIM)], wl.at[0]),
        pltpu.make_async_copy(wv_h, wkv.at[:, pl.ds(HDIM, HDIM)], wl.at[1]),
        pltpu.make_async_copy(wq_h, wq, wl.at[2]),
        pltpu.make_async_copy(wo_h, wo, wl.at[3]),
    ]

    @pl.when(own)
    def _():
        for copy in local:
            copy.start()

    anc_local = pltpu.make_async_copy(anc_h, anc_s.at[k], an_l.at[0])
    anc_local.start()

    def rows_of(core, first, count):
        return pl.ds(pl.multiple_of(core * BLOCK + first, HALF), count)

    @pl.loop(0, BLOCK // 16)
    def _(i):
        rows = pl.ds(pl.multiple_of(i * 16, 16), 16)
        v = hid[rows, :].astype(F32)
        scale = lax.rsqrt(jnp.mean(v * v, axis=1, keepdims=True) + 1e-06)
        xb[0, pl.ds(pl.multiple_of(k * BLOCK + i * 16, 16), 16), :] = (v * scale * gain[...]).astype(BF16)

    pl.semaphore_wait(barrier, len(greeted))

    A, B = (0, HALF), (HALF, HALF)
    routes = [
        (0, 1, A, right), (0, 1, B, right), (0, 3, B, left), (0, 3, A, left), (0, 0, (0, BLOCK), sib),
        (1, 2, A, right), (3, 2, B, left),
        (1, 1, A, sib), (1, 1, B, sib), (3, 3, B, sib), (3, 3, A, sib), (2, 2, A, sib), (2, 2, B, sib),
    ]

    def ag(m):
        s, t, (first, count), to = routes[m]
        rows = rows_of(k, first, count)
        return send(xb.at[s, rows, :], xb.at[t, rows, :], ag_s.at[m], ag_r.at[m], to)

    for m in range(5):
        ag(m).start()

    anc_send = send(anc_h, anc_v, an_s.at[0], an_r.at[0], sib)
    anc_send.start()

    def chunk(n, quarter):
        def rows(size, part, parts):
            return pl.ds(pl.multiple_of(quarter * size + part * (size // parts), 16), size // parts)

        if n == 0:
            r = rows(D // 4, 0, 1)
            return wk_h.at[r, :], wkv.at[r, pl.ds(0, HDIM)]
        if n == 1:
            r = rows(D // 4, 0, 1)
            return wv_h.at[r, :], wkv.at[r, pl.ds(HDIM, HDIM)]
        if n in (2, 3):
            r = rows(D // 4, n - 2, 2)
            return wq_h.at[r, :], wq.at[r, :]
        r = rows(QCOLS // 4, 0, 1)
        cols = pl.ds((n - 4) * WIDE, WIDE)
        return wo_h.at[r, cols], wo.at[r, cols]

    y_target = dev(x, (y + 3 + 2 * k) % 4, z, par)

    def w_out_send(n):
        quarter = 2 * zp + k
        src, dst = chunk(n, quarter)
        return send(src, dst, ws_s.at[n], ws_r.at[n, quarter], y_target)

    def w_arrival(n, quarter):
        _, dst = chunk(n, quarter)
        return send(dst, dst, ws_s.at[n], ws_r.at[n, quarter], y_target)

    def w_pass(n, side):
        quarter = 2 * zp + side
        _, dst = chunk(n, quarter)
        to = dev(x, y, (z + 1 + 2 * side) % 4, k)
        return send(dst, dst, wz_s.at[n, side], ws_r.at[n, quarter], to)

    def pass_weights(chunks):
        @pl.when(jnp.logical_not(own))
        def _():
            for n in chunks:
                for side in range(2):
                    w_arrival(n, 2 * zp + side).wait_recv()
                    w_pass(n, side).start()

    def wait_weights(chunks, locals_):
        @pl.when(own)
        def _():
            for i in locals_:
                local[i].wait()

        @pl.when(jnp.logical_not(own))
        def _():
            for n in chunks:
                for side in range(2):
                    w_arrival(n, 2 * (1 - zp) + side).wait_recv()

    for n in range(6):
        w_out_send(n).start()

    pass_weights((0, 1))

    def rope(block):
        cos_b, sin_b = cb[pl.ds(block, 1), :], sb[pl.ds(block, 1), :]
        cosine = cos_b * ci[...] - sin_b * si[...]
        sine = sin_b * ci[...] + cos_b * si[...]
        lane = lax.broadcasted_iota(jnp.int32, (BLOCK, HDIM), 1)
        return cosine, jnp.where(lane < HDIM // 2, -sine, sine)

    def rotated(v, table):
        return v * table[0] + pltpu.roll(v, HDIM // 2, 1) * table[1]

    def x_of(r):
        return (x + 4 - r) % 4

    def block_of(r, core):
        return 16 * span + 8 * core + 2 * x_of(r) + par

    def project_kv(r):
        both = jnp.dot(xb[r], wkv[...], preferred_element_type=F32)
        for core in range(2):
            part = both[core * BLOCK : (core + 1) * BLOCK]
            slot = 48 + 8 * par + 2 * x_of(r) + core
            kv[slot, 0] = rotated(part[:, :HDIM], rope(block_of(r, core))).astype(BF16)
            kv[slot, 1] = part[:, HDIM:].astype(BF16)

    def project_q(r):
        for first, count in ((0, 2), (2, 2), (4, 1)):
            got = jnp.dot(xb[r], wq[:, first * HDIM : (first + count) * HDIM], preferred_element_type=F32)
            for core in range(2):
                table = rope(block_of(r, core))
                for e in range(count):
                    part = got[core * BLOCK : (core + 1) * BLOCK, e * HDIM : (e + 1) * HDIM]
                    qs[r, core, first + e] = (rotated(part, table) * Q_SCALE).astype(BF16)

    def kv_pair(region, parity, r):
        return kv.at[pl.ds(16 * region + 8 * parity + 2 * x_of(r), 2)]

    def kv_send(n, src, dst, parity, r, to):
        return send(
            kv_pair(src, parity, r), kv_pair(dst, parity, r), kv_s.at[n], kv_r.at[dst * 8 + parity * 4 + r], to
        )

    def kv_up(r):
        return kv_send(r, 3, 1, par, r, above)

    def kv_partner(r, region):
        return kv_send((16 if region == 1 else 4) + r, region, region, par, r, partner)

    def kv_opposite(region):
        return kv_send(32 + region // 3, region, 2, par, 2, opposite)

    def kv_cross(r, region, mine):
        parity = par if mine else 1 - par
        return kv_send((20 if region == 1 else 8) + 2 * r + mine, region, 2, parity, r, cross)

    def kv_from_partner(r, region):
        return kv_send(0, region, region, 1 - par, r, partner)

    def kv_far(i, t):
        slot = 8 * par + 5 + 2 * i
        to = dev(x, (cross_y, opposite_y)[t], (z + yh) % 4, k)
        return send(
            kv.at[pl.ds(16 + slot, 1)], kv.at[pl.ds(slot, 1)],
            kv_s.at[28 + 2 * i + t], kv_r.at[par * 4 + i], to,
        )

    far_sends = jnp.logical_and(z > 0, z + yh < 4)

    def start_kv(r):
        @pl.when(z < 3)
        def _():
            kv_up(r).start()

        kv_partner(r, 3).start()

        @pl.when(yh == 0)
        def _():
            kv_cross(r, 3, 1).start()
            if r == 2:
                kv_opposite(3).start()

    def pass_kv(r):
        @pl.when(z > 0)
        def _():
            kv_up(r).wait_recv()
            kv_partner(r, 1).start()

            @pl.when(yh == 1)
            def _():
                kv_cross(r, 1, 1).start()
                if r == 2:
                    kv_opposite(1).start()

    def pass_partner_kv(r):
        kv_from_partner(r, 3).wait_recv()

        @pl.when(yh == 0)
        def _():
            kv_cross(r, 3, 0).start()

        @pl.when(z > 0)
        def _():
            kv_from_partner(r, 1).wait_recv()

            @pl.when(yh == 1)
            def _():
                kv_cross(r, 1, 0).start()

    ag(0).wait_recv()
    ag(5).start()
    ag(7).start()
    ag(2).wait_recv()
    ag(6).start()
    ag(9).start()
    pass_weights((2, 3))
    wait_weights((0, 1), (0, 1))
    ag(4).wait_recv()
    project_kv(0)
    ag(1).wait_recv()
    ag(8).start()
    ag(3).wait_recv()
    ag(10).start()
    for m in (7, 8, 9, 10):
        ag(m).wait_recv()

    @pl.loop(0, 2)
    def _(i):
        project_kv(1 + 2 * i)

    for r in (0, 1, 3):
        start_kv(r)
    pass_weights((4,))
    wait_weights((2, 3), (2,))

    @pl.loop(0, 3)
    def _(i):
        project_q(i + i // 2)

    for r in (0, 1, 3):
        pass_kv(r)
    for r in (0, 1, 3):
        pass_partner_kv(r)
    for m in (5, 6):
        ag(m).wait_recv()
        ag(m + 6).start()
    for m in (11, 12):
        ag(m).wait_recv()
    project_kv(2)
    start_kv(2)
    project_q(2)
    pass_kv(2)

    @pl.when(far_sends)
    def _():
        for i in range(2):
            for t in range(2):
                kv_far(i, t).start()

    pass_weights((5,))
    for m in range(13):
        ag(m).wait_send()

    anc_local.wait()
    anc_send.wait()
    anc_move = pltpu.make_async_copy(anc_v, anc_s.at[1 - k], an_l.at[1])
    anc_move.start()
    anc_move.wait()

    def kv_arrival(region, parity, r, blocks):
        ref = kv.at[pl.ds(16 * region + 8 * parity + 2 * r, blocks)]
        return send(ref, ref, kv_s.at[0], kv_r.at[region * 8 + parity * 4 + r], partner)

    kv_from_partner(2, 3).wait_recv()

    @pl.when(z > 0)
    def _():
        kv_from_partner(2, 1).wait_recv()

    @pl.when(span >= 1)
    def _():
        for parity in range(2):
            for r in range(4):
                kv_arrival(2, parity, r, 2).wait_recv()

    @pl.when(span >= 3)
    def _():
        for parity in range(2):
            for i in range(2):
                kv_arrival(0, parity, i, 1).wait_recv()

    def attend(r):
        xr = x_of(r)

        @pl.loop(0, 2)
        def _(core):
            row = 2 * xr + par
            mine = 48 + 8 * par + 2 * xr + core
            keys, values, biases = [kv[mine, 0]], [kv[mine, 1]], [None]
            for j in range(MAXA):
                a = anc_s[core, row, j]
                listed = a >= 0
                place = jnp.where(listed, jnp.clip(a - 16 * span + 48, 0, 63), 48 + 8 * core + row)
                within = place % 16
                slot = (place // 16) * 16 + (within % 2) * 8 + ((within // 2) % 4) * 2 + within // 8
                keys.append(kv[slot, 0])
                values.append(kv[slot, 1])
                biases.append(jnp.where(listed, 0.0, -1e30).astype(F32))
            causal = lax.broadcasted_iota(jnp.int32, (BLOCK, BLOCK), 0) >= lax.broadcasted_iota(
                jnp.int32, (BLOCK, BLOCK), 1
            )
            for e in range(PER_GROUP):
                q = qs[r, core, e]
                scores = []
                for key, bias in zip(keys, biases):
                    s = lax.dot_general(q, key, (((1,), (1,)), ((), ())), preferred_element_type=F32)
                    scores.append(jnp.where(causal, s, -1e30) if bias is None else s + bias)
                top = functools.reduce(jnp.maximum, scores).max(axis=1, keepdims=True)
                weights = [jnp.exp2(s - top) for s in scores]
                total = functools.reduce(jnp.add, weights).sum(axis=1, keepdims=True)
                mixture = sum(
                    jnp.dot(w.astype(BF16), v, preferred_element_type=F32) for w, v in zip(weights, values)
                )
                att[r, rows_of(core, 0, BLOCK), e * HDIM : (e + 1) * HDIM] = (mixture / total).astype(BF16)

    def wide(j):
        return pl.ds(j * WIDE, WIDE)

    def project_out(r, j):
        @pl.loop(0, WIDE // N_OUT)
        def _(n):
            cols = pl.ds(pl.multiple_of(j * WIDE + n * N_OUT, N_OUT), N_OUT)
            xb[r, :, cols] = jnp.dot(att[r], wo[:, cols], preferred_element_type=F32).astype(BF16)

    def to_sibling(r, j):
        n = 4 * j + r
        src = xb.at[r, rows_of(1 - k, 0, BLOCK), wide(j)]
        return send(src, rb.at[r, :, wide(j)], rs_s.at[n], rs_r.at[n], sib)

    def add_into(r, j, first, count, term):
        @pl.loop(0, count // 16)
        def _(i):
            at = pl.ds(pl.multiple_of(i * 16, 16), 16)
            rows = pl.ds(pl.multiple_of(k * BLOCK + first + i * 16, 16), 16)
            total = xb[r, rows, wide(j)].astype(F32) + term[at, wide(j)].astype(F32)
            xb[r, rows, wide(j)] = total.astype(BF16)

    def half(r, j, first):
        return xb.at[r, rows_of(k, first, HALF), wide(j)]

    def far_send(side, j):
        n = 8 + 2 * j + side
        return send(half(2, j, side * HALF), far.at[side, :, wide(j)], rs_s.at[n], rs_r.at[n], (right, left)[side])

    def fin_send(side, j, first):
        n = 12 + 4 * j + 2 * side + first // HALF
        dst = fin.at[side, pl.ds(first, HALF), wide(j)]
        return send(half((3, 1)[side], j, first), dst, rs_s.at[n], rs_r.at[n], (right, left)[side])

    def take_sibling(r, j):
        to_sibling(r, j).wait_recv()
        add_into(r, j, 0, BLOCK, rb.at[r])

    def put_out(r, j):
        project_out(r, j)
        to_sibling(r, j).start()

    def open_half(j, attend):
        put_out(2, j)
        attend(3)
        take_sibling(2, j)
        for side in range(2):
            far_send(side, j).start()
        put_out(3, j)
        attend(1)
        put_out(1, j)
        take_sibling(3, j)
        fin_send(0, j, HALF).start()
        take_sibling(1, j)
        fin_send(1, j, 0).start()
        attend(0)
        put_out(0, j)

    def close_half(j):
        for side, r, first in ((0, 3, 0), (1, 1, HALF)):
            far_send(side, j).wait_recv()
            add_into(r, j, first, HALF, far.at[side])
            fin_send(side, j, first).start()

    def finish(j):
        to_sibling(0, j).wait_recv()
        for side, first in ((0, HALF), (1, 0), (0, 0), (1, HALF)):
            fin_send(side, j, first).wait_recv()

        @pl.loop(0, BLOCK // 16)
        def _(i):
            at = pl.ds(pl.multiple_of(i * 16, 16), 16)
            rows = pl.ds(pl.multiple_of(k * BLOCK + i * 16, 16), 16)
            total = xb[0, rows, wide(j)].astype(F32) + rb[0, at, wide(j)].astype(F32)
            total = total + fin[0, at, wide(j)].astype(F32) + fin[1, at, wide(j)].astype(F32)
            out[at, wide(j)] = total.astype(BF16)

    attend(2)
    wait_weights((4,), (3,))
    open_half(0, attend)
    close_half(0)
    wait_weights((5,), ())
    open_half(1, lambda r: None)
    finish(0)
    close_half(1)
    finish(1)

    for r in range(4):
        for j in range(2):
            to_sibling(r, j).wait_send()
        kv_partner(r, 3).wait_send()
    for j in range(2):
        for side in range(2):
            far_send(side, j).wait_send()
            for first in (0, HALF):
                fin_send(side, j, first).wait_send()
    for n in range(6):
        w_out_send(n).wait_send()

    @pl.when(jnp.logical_not(own))
    def _():
        for n in range(6):
            for side in range(2):
                w_pass(n, side).wait_send()

    @pl.when(z < 3)
    def _():
        for r in range(4):
            kv_up(r).wait_send()

    @pl.when(yh == 0)
    def _():
        kv_opposite(3).wait_send()
        for r in range(4):
            for mine in range(r == 2, 2):
                kv_cross(r, 3, mine).wait_send()

    @pl.when(z > 0)
    def _():
        for r in range(4):
            kv_partner(r, 1).wait_send()

    @pl.when(jnp.logical_and(z > 0, yh == 1))
    def _():
        kv_opposite(1).wait_send()
        for r in range(4):
            for mine in range(r == 2, 2):
                kv_cross(r, 1, mine).wait_send()

    @pl.when(far_sends)
    def _():
        for i in range(2):
            for t in range(2):
                kv_far(i, t).wait_send()


def on_device(hidden_rows, norm_gain, w_query, w_key, w_value, w_out, ancestors):
    vmem = pl.BlockSpec(memory_space=pltpu.VMEM)
    hbm = pl.BlockSpec(memory_space=pl.ANY)
    dma = pltpu.SemaphoreType.DMA
    lists = jnp.pad(ancestors, ((0, 0), (0, 128 - MAXA)))
    return pl.pallas_call(
        kernel,
        out_shape=jax.ShapeDtypeStruct((BLOCK, D), BF16),
        in_specs=[vmem, vmem, hbm, hbm, hbm, hbm, hbm, vmem, vmem, vmem, vmem],
        out_specs=vmem,
        scratch_shapes=[
            pltpu.VMEM((4, 2 * BLOCK, D), BF16),
            pltpu.VMEM((D, 2 * HDIM), BF16),
            pltpu.VMEM((D, QCOLS), BF16),
            pltpu.VMEM((QCOLS, D), BF16),
            pltpu.VMEM((4, 2, PER_GROUP, BLOCK, HDIM), BF16),
            pltpu.VMEM((64, 2, BLOCK, HDIM), BF16),
            pltpu.VMEM((4, 2 * BLOCK, QCOLS), BF16),
            pltpu.VMEM((4, BLOCK, D), BF16),
            pltpu.VMEM((2, HALF, D), BF16),
            pltpu.VMEM((2, BLOCK, D), BF16),
            pltpu.VMEM((8, 128), jnp.int32),
            pltpu.SMEM((2, 8, 128), jnp.int32),
            dma((13,)),
            dma((13,)),
            dma((6,)),
            dma((6, 4)),
            dma((6, 2)),
            dma((4,)),
            dma((34,)),
            dma((32,)),
            dma((20,)),
            dma((20,)),
            dma((1,)),
            dma((1,)),
            dma((2,)),
        ],
        compiler_params=pltpu.CompilerParams(
            collective_id=0, has_side_effects=True, vmem_limit_bytes=60 * 2**20
        ),
        cost_estimate=pl.CostEstimate(
            flops=17 * 10**9, bytes_accessed=20 * 10**6, transcendentals=4 * 10**6
        ),
    )(
        hidden_rows, norm_gain.reshape(1, D), w_query, w_key, w_value, w_out, lists,
        *[jnp.asarray(t) for t in rope_tables()],
    )


def solution(mesh):
    placed = (
        P(("ctx", "head"), None),
        P(),
        P(None, "head"),
        P(None, "head"),
        P(None, "head"),
        P("head", None),
        P("ctx", None),
    )
    return jax.shard_map(
        on_device, mesh=mesh, in_specs=placed, out_specs=P(("ctx", "head"), None), check_vma=False
    )
```

```python
import functools

import jax
import jax.numpy as jnp
import numpy as np
from jax import lax
from jax.experimental import pallas as pl
from jax.experimental.pallas import tpu as pltpu
from jax.sharding import PartitionSpec as P

D = 5120
HDIM = 128
BLOCK = 128
MAXA = 4
PER_GROUP = 5
QCOLS = PER_GROUP * HDIM
HALF = BLOCK // 2
ROPE_BASE = 1000000.0
Q_SCALE = float(HDIM**-0.5 * np.log2(np.e))
MESH = pl.DeviceIdType.MESH
F32 = jnp.float32
BF16 = jnp.bfloat16
N_OUT = 1280
WIDE = D // 2
ROWS = 64


def rope_tables():
    frequency = ROPE_BASE ** (-2.0 * np.arange(HDIM // 2) / HDIM)
    frequency = np.concatenate([frequency, frequency])
    inner = np.arange(BLOCK)[:, None] * frequency[None, :]
    outer = np.arange(128)[:, None] * float(BLOCK) * frequency[None, :]
    return [f(t).astype(np.float32) for t in (inner, outer) for f in (np.cos, np.sin)]


def kernel(
    hid, gain, wq_h, wk_h, wv_h, wo_h, anc_h, ci, si, cb, sb,
    out,
    xb, wkv, wq, wo, qs, kv, att, rb, far, fin, kc, vc, scores, probs, share, anc_v, anc_s,
    ag_s, ag_r, ws_s, ws_r, wz_s, wl, kv_s, kv_r, rs_s, rs_r, an_s, an_r, an_l,
):
    c = lax.axis_index("ctx")
    h = lax.axis_index("head")
    x = h // 2
    par = h % 2
    yh = (c // 2) % 2
    z = c // 4
    k = c % 2
    y = yh * 2 + par
    zp = z % 2
    span = 2 * z + yh
    own = k == par

    def dev(x, y, z, k):
        return {"ctx": z * 4 + (y // 2) * 2 + k, "head": x * 2 + y % 2}

    right = dev((x + 1) % 4, y, z, k)
    left = dev((x + 3) % 4, y, z, k)
    sib = dev(x, y, z, 1 - k)

    def send(src, dst, ssem, rsem, to):
        return pltpu.make_async_remote_copy(
            src_ref=src, dst_ref=dst, send_sem=ssem, recv_sem=rsem, device_id=to, device_id_type=MESH
        )

    barrier = pltpu.get_barrier_semaphore()
    partner = dev(x, yh * 2 + 1 - par, z, k)
    cross_y = (1 - yh) * 2 + 1 - par
    cross = dev(x, cross_y, z, k)
    above = dev(x, y, (z + 1) % 4, k)
    greeted = [right, left, sib, partner, cross, above, dev(x, y, (z + 3) % 4, k)]
    greeted += [dev(x, (y + d) % 4, z, 1 - k) for d in (1, 3)]
    opposite_y = (1 - yh) * 2 + par
    opposite = dev(x, opposite_y, z, k)
    next_z = (z + 3 + 2 * yh) % 4
    greeted += [opposite, dev(x, cross_y, next_z, k), dev(x, opposite_y, next_z, k)]
    for to in greeted:
        pl.semaphore_signal(barrier, 1, device_id=to, device_id_type=MESH)

    local = [
        pltpu.make_async_copy(wk_h, wkv.at[:, pl.ds(0, HDIM)], wl.at[0]),
        pltpu.make_async_copy(wv_h, wkv.at[:, pl.ds(HDIM, HDIM)], wl.at[1]),
        pltpu.make_async_copy(wq_h, wq, wl.at[2]),
        pltpu.make_async_copy(wo_h, wo, wl.at[3]),
    ]

    @pl.when(own)
    def _():
        for copy in local:
            copy.start()

    anc_local = pltpu.make_async_copy(anc_h, anc_s.at[k], an_l.at[0])
    anc_local.start()

    def rows_of(core, first, count):
        return pl.ds(pl.multiple_of(core * BLOCK + first, HALF), count)

    @pl.loop(0, BLOCK // 16)
    def _(i):
        rows = pl.ds(pl.multiple_of(i * 16, 16), 16)
        v = hid[rows, :].astype(F32)
        scale = lax.rsqrt(jnp.mean(v * v, axis=1, keepdims=True) + 1e-06)
        xb[0, pl.ds(pl.multiple_of(k * BLOCK + i * 16, 16), 16), :] = (v * scale * gain[...]).astype(BF16)

    pl.semaphore_wait(barrier, len(greeted))

    A, B = (0, HALF), (HALF, HALF)
    routes = [
        (0, 1, A, right), (0, 1, B, right), (0, 3, B, left), (0, 3, A, left), (0, 0, (0, BLOCK), sib),
        (1, 2, A, right), (3, 2, B, left),
        (1, 1, A, sib), (1, 1, B, sib), (3, 3, B, sib), (3, 3, A, sib), (2, 2, A, sib), (2, 2, B, sib),
    ]

    def ag(m):
        s, t, (first, count), to = routes[m]
        rows = rows_of(k, first, count)
        return send(xb.at[s, rows, :], xb.at[t, rows, :], ag_s.at[m], ag_r.at[m], to)

    for m in range(5):
        ag(m).start()

    anc_send = send(anc_h, anc_v, an_s.at[0], an_r.at[0], sib)
    anc_send.start()

    def chunk(n, quarter):
        def rows(size, part, parts):
            return pl.ds(pl.multiple_of(quarter * size + part * (size // parts), 16), size // parts)

        if n == 0:
            r = rows(D // 4, 0, 1)
            return wk_h.at[r, :], wkv.at[r, pl.ds(0, HDIM)]
        if n == 1:
            r = rows(D // 4, 0, 1)
            return wv_h.at[r, :], wkv.at[r, pl.ds(HDIM, HDIM)]
        if n in (2, 3):
            r = rows(D // 4, n - 2, 2)
            return wq_h.at[r, :], wq.at[r, :]
        r = rows(QCOLS // 4, 0, 1)
        cols = pl.ds((n - 4) * WIDE, WIDE)
        return wo_h.at[r, cols], wo.at[r, cols]

    y_target = dev(x, (y + 3 + 2 * k) % 4, z, par)

    def w_out_send(n):
        quarter = 2 * zp + k
        src, dst = chunk(n, quarter)
        return send(src, dst, ws_s.at[n], ws_r.at[n, quarter], y_target)

    def w_arrival(n, quarter):
        _, dst = chunk(n, quarter)
        return send(dst, dst, ws_s.at[n], ws_r.at[n, quarter], y_target)

    def w_pass(n, side):
        quarter = 2 * zp + side
        _, dst = chunk(n, quarter)
        to = dev(x, y, (z + 1 + 2 * side) % 4, k)
        return send(dst, dst, wz_s.at[n, side], ws_r.at[n, quarter], to)

    def pass_weights(chunks):
        @pl.when(jnp.logical_not(own))
        def _():
            for n in chunks:
                for side in range(2):
                    w_arrival(n, 2 * zp + side).wait_recv()
                    w_pass(n, side).start()

    def wait_weights(chunks, locals_):
        @pl.when(own)
        def _():
            for i in locals_:
                local[i].wait()

        @pl.when(jnp.logical_not(own))
        def _():
            for n in chunks:
                for side in range(2):
                    w_arrival(n, 2 * (1 - zp) + side).wait_recv()

    for n in range(6):
        w_out_send(n).start()

    pass_weights((0, 1))

    def rope(block):
        cos_b, sin_b = cb[pl.ds(block, 1), :], sb[pl.ds(block, 1), :]
        cosine = cos_b * ci[...] - sin_b * si[...]
        sine = sin_b * ci[...] + cos_b * si[...]
        lane = lax.broadcasted_iota(jnp.int32, (BLOCK, HDIM), 1)
        return cosine, jnp.where(lane < HDIM // 2, -sine, sine)

    def rotated(v, table):
        return v * table[0] + pltpu.roll(v, HDIM // 2, 1) * table[1]

    def x_of(r):
        return (x + 4 - r) % 4

    def block_of(r, core):
        return 16 * span + 8 * core + 2 * x_of(r) + par

    def project_kv(r):
        both = jnp.dot(xb[r], wkv[...], preferred_element_type=F32)
        for core in range(2):
            part = both[core * BLOCK : (core + 1) * BLOCK]
            slot = 48 + 8 * par + 2 * x_of(r) + core
            kv[slot, 0] = rotated(part[:, :HDIM], rope(block_of(r, core))).astype(BF16)
            kv[slot, 1] = part[:, HDIM:].astype(BF16)

    def project_q(r):
        for first, count in ((0, 2), (2, 2), (4, 1)):
            got = jnp.dot(xb[r], wq[:, first * HDIM : (first + count) * HDIM], preferred_element_type=F32)
            for core in range(2):
                table = rope(block_of(r, core))
                for e in range(count):
                    part = got[core * BLOCK : (core + 1) * BLOCK, e * HDIM : (e + 1) * HDIM]
                    qs[r, core, first + e] = (rotated(part, table) * Q_SCALE).astype(BF16)

    def kv_pair(region, parity, r):
        return kv.at[pl.ds(16 * region + 8 * parity + 2 * x_of(r), 2)]

    def kv_send(n, src, dst, parity, r, to):
        return send(
            kv_pair(src, parity, r), kv_pair(dst, parity, r), kv_s.at[n], kv_r.at[dst * 8 + parity * 4 + r], to
        )

    def kv_up(r):
        return kv_send(r, 3, 1, par, r, above)

    def kv_partner(r, region):
        return kv_send((16 if region == 1 else 4) + r, region, region, par, r, partner)

    def kv_opposite(region):
        return kv_send(32 + region // 3, region, 2, par, 2, opposite)

    def kv_cross(r, region, mine):
        parity = par if mine else 1 - par
        return kv_send((20 if region == 1 else 8) + 2 * r + mine, region, 2, parity, r, cross)

    def kv_from_partner(r, region):
        return kv_send(0, region, region, 1 - par, r, partner)

    def kv_far(i, t):
        slot = 8 * par + 5 + 2 * i
        to = dev(x, (cross_y, opposite_y)[t], (z + yh) % 4, k)
        return send(
            kv.at[pl.ds(16 + slot, 1)], kv.at[pl.ds(slot, 1)],
            kv_s.at[28 + 2 * i + t], kv_r.at[par * 4 + i], to,
        )

    far_sends = jnp.logical_and(z > 0, z + yh < 4)

    def start_kv(r):
        @pl.when(z < 3)
        def _():
            kv_up(r).start()

        kv_partner(r, 3).start()

        @pl.when(yh == 0)
        def _():
            kv_cross(r, 3, 1).start()
            if r == 2:
                kv_opposite(3).start()

    def pass_kv(r):
        @pl.when(z > 0)
        def _():
            kv_up(r).wait_recv()
            kv_partner(r, 1).start()

            @pl.when(yh == 1)
            def _():
                kv_cross(r, 1, 1).start()
                if r == 2:
                    kv_opposite(1).start()

    def pass_partner_kv(r):
        kv_from_partner(r, 3).wait_recv()

        @pl.when(yh == 0)
        def _():
            kv_cross(r, 3, 0).start()

        @pl.when(z > 0)
        def _():
            kv_from_partner(r, 1).wait_recv()

            @pl.when(yh == 1)
            def _():
                kv_cross(r, 1, 0).start()

    ag(0).wait_recv()
    ag(5).start()
    ag(7).start()
    ag(2).wait_recv()
    ag(6).start()
    ag(9).start()
    pass_weights((2, 3))
    wait_weights((0, 1), (0, 1))
    ag(4).wait_recv()
    project_kv(0)
    ag(1).wait_recv()
    ag(8).start()
    ag(3).wait_recv()
    ag(10).start()
    for m in (7, 8, 9, 10):
        ag(m).wait_recv()

    @pl.loop(0, 2)
    def _(i):
        project_kv(1 + 2 * i)

    for r in (0, 1, 3):
        start_kv(r)
    pass_weights((4,))
    wait_weights((2, 3), (2,))

    project_q(0)
    for r in (0, 1, 3):
        pass_kv(r)
    project_q(1)
    for m in (5, 6):
        ag(m).wait_recv()
        ag(m + 6).start()
    for m in (11, 12):
        ag(m).wait_recv()
    project_kv(2)
    start_kv(2)
    for r in (0, 1, 3):
        pass_partner_kv(r)
    pass_kv(2)

    @pl.when(far_sends)
    def _():
        for i in range(2):
            for t in range(2):
                kv_far(i, t).start()

    pass_weights((5,))

    @pl.loop(2, 4)
    def _(i):
        project_q(i)

    for m in range(13):
        ag(m).wait_send()

    anc_local.wait()
    anc_send.wait()
    anc_move = pltpu.make_async_copy(anc_v, anc_s.at[1 - k], an_l.at[1])
    anc_move.start()
    anc_move.wait()

    def kv_arrival(region, parity, r, blocks):
        ref = kv.at[pl.ds(16 * region + 8 * parity + 2 * r, blocks)]
        return send(ref, ref, kv_s.at[0], kv_r.at[region * 8 + parity * 4 + r], partner)

    kv_from_partner(2, 3).wait_recv()

    @pl.when(z > 0)
    def _():
        kv_from_partner(2, 1).wait_recv()

    @pl.when(span >= 1)
    def _():
        for parity in range(2):
            for r in range(4):
                kv_arrival(2, parity, r, 2).wait_recv()

    @pl.when(span >= 3)
    def _():
        for parity in range(2):
            for i in range(2):
                kv_arrival(0, parity, i, 1).wait_recv()

    def attend(r):
        xr = x_of(r)

        @pl.loop(0, 2)
        def _(core):
            row = 2 * xr + par
            mine = 48 + 8 * par + 2 * xr + core
            kc[0:BLOCK, :] = kv[mine, 0]
            vc[0:BLOCK, :] = kv[mine, 1]
            biases = []
            for j in range(MAXA):
                a = anc_s[core, row, j]
                listed = a >= 0
                place = jnp.where(listed, jnp.clip(a - 16 * span + 48, 0, 63), 48 + 8 * core + row)
                within = place % 16
                slot = (place // 16) * 16 + (within % 2) * 8 + ((within // 2) % 4) * 2 + within // 8
                kc[(j + 1) * BLOCK : (j + 2) * BLOCK, :] = kv[slot, 0]
                vc[(j + 1) * BLOCK : (j + 2) * BLOCK, :] = kv[slot, 1]
                biases.append(jnp.where(listed, 0.0, -1e30).astype(F32))
            q = qs[r, core].reshape(QCOLS, HDIM)
            scores[...] = lax.dot_general(q, kc[...], (((1,), (1,)), ((), ())), preferred_element_type=F32)
            for first in range(0, QCOLS, ROWS):
                rows = slice(first, first + ROWS)
                causal = lax.broadcasted_iota(jnp.int32, (ROWS, BLOCK), 0) + first % BLOCK >= (
                    lax.broadcasted_iota(jnp.int32, (ROWS, BLOCK), 1)
                )
                parts = [jnp.where(causal, scores[rows, 0:BLOCK], -1e30)]
                for j in range(MAXA):
                    parts.append(scores[rows, (j + 1) * BLOCK : (j + 2) * BLOCK] + biases[j])
                top = functools.reduce(jnp.maximum, parts).max(axis=1, keepdims=True)
                parts = [jnp.exp2(part - top) for part in parts]
                total = functools.reduce(jnp.add, parts).sum(axis=1, keepdims=True)
                share[rows, :] = jnp.broadcast_to(1.0 / total, (ROWS, HDIM))
                for j in range(MAXA + 1):
                    probs[rows, j * BLOCK : (j + 1) * BLOCK] = parts[j].astype(BF16)
            mixture = jnp.dot(probs[...], vc[...], preferred_element_type=F32) * share[...]
            for e in range(PER_GROUP):
                att[r, rows_of(core, 0, BLOCK), e * HDIM : (e + 1) * HDIM] = mixture[
                    e * BLOCK : (e + 1) * BLOCK
                ].astype(BF16)

    def wide(j):
        return pl.ds(j * WIDE, WIDE)

    def project_out(r, j):
        @pl.loop(0, WIDE // N_OUT)
        def _(n):
            cols = pl.ds(pl.multiple_of(j * WIDE + n * N_OUT, N_OUT), N_OUT)
            xb[r, :, cols] = jnp.dot(att[r], wo[:, cols], preferred_element_type=F32).astype(BF16)

    def to_sibling(r, j):
        n = 4 * j + r
        src = xb.at[r, rows_of(1 - k, 0, BLOCK), wide(j)]
        return send(src, rb.at[r, :, wide(j)], rs_s.at[n], rs_r.at[n], sib)

    def add_into(r, j, first, count, term):
        @pl.loop(0, count // 16)
        def _(i):
            at = pl.ds(pl.multiple_of(i * 16, 16), 16)
            rows = pl.ds(pl.multiple_of(k * BLOCK + first + i * 16, 16), 16)
            total = xb[r, rows, wide(j)].astype(F32) + term[at, wide(j)].astype(F32)
            xb[r, rows, wide(j)] = total.astype(BF16)

    def half(r, j, first):
        return xb.at[r, rows_of(k, first, HALF), wide(j)]

    def far_send(side, j):
        n = 8 + 2 * j + side
        return send(half(2, j, side * HALF), far.at[side, :, wide(j)], rs_s.at[n], rs_r.at[n], (right, left)[side])

    def fin_send(side, j, first):
        n = 12 + 4 * j + 2 * side + first // HALF
        dst = fin.at[side, pl.ds(first, HALF), wide(j)]
        return send(half((3, 1)[side], j, first), dst, rs_s.at[n], rs_r.at[n], (right, left)[side])

    def take_sibling(r, j):
        to_sibling(r, j).wait_recv()
        add_into(r, j, 0, BLOCK, rb.at[r])

    def put_out(r, j):
        project_out(r, j)
        to_sibling(r, j).start()

    def open_half(j, attend):
        put_out(2, j)
        attend(3)
        take_sibling(2, j)
        for side in range(2):
            far_send(side, j).start()
        put_out(3, j)
        attend(1)
        put_out(1, j)
        take_sibling(3, j)
        fin_send(0, j, HALF).start()
        take_sibling(1, j)
        fin_send(1, j, 0).start()
        attend(0)
        put_out(0, j)

    def close_half(j):
        for side, r, first in ((0, 3, 0), (1, 1, HALF)):
            far_send(side, j).wait_recv()
            add_into(r, j, first, HALF, far.at[side])
            fin_send(side, j, first).start()

    def finish(j):
        to_sibling(0, j).wait_recv()
        for side, first in ((0, HALF), (1, 0), (0, 0), (1, HALF)):
            fin_send(side, j, first).wait_recv()

        @pl.loop(0, BLOCK // 16)
        def _(i):
            at = pl.ds(pl.multiple_of(i * 16, 16), 16)
            rows = pl.ds(pl.multiple_of(k * BLOCK + i * 16, 16), 16)
            total = xb[0, rows, wide(j)].astype(F32) + rb[0, at, wide(j)].astype(F32)
            total = total + fin[0, at, wide(j)].astype(F32) + fin[1, at, wide(j)].astype(F32)
            out[at, wide(j)] = total.astype(BF16)

    attend(2)
    wait_weights((4,), (3,))
    open_half(0, attend)
    close_half(0)
    wait_weights((5,), ())
    open_half(1, lambda r: None)
    finish(0)
    close_half(1)
    finish(1)

    for r in range(4):
        for j in range(2):
            to_sibling(r, j).wait_send()
        kv_partner(r, 3).wait_send()
    for j in range(2):
        for side in range(2):
            far_send(side, j).wait_send()
            for first in (0, HALF):
                fin_send(side, j, first).wait_send()
    for n in range(6):
        w_out_send(n).wait_send()

    @pl.when(jnp.logical_not(own))
    def _():
        for n in range(6):
            for side in range(2):
                w_pass(n, side).wait_send()

    @pl.when(z < 3)
    def _():
        for r in range(4):
            kv_up(r).wait_send()

    @pl.when(yh == 0)
    def _():
        kv_opposite(3).wait_send()
        for r in range(4):
            for mine in range(r == 2, 2):
                kv_cross(r, 3, mine).wait_send()

    @pl.when(z > 0)
    def _():
        for r in range(4):
            kv_partner(r, 1).wait_send()

    @pl.when(jnp.logical_and(z > 0, yh == 1))
    def _():
        kv_opposite(1).wait_send()
        for r in range(4):
            for mine in range(r == 2, 2):
                kv_cross(r, 1, mine).wait_send()

    @pl.when(far_sends)
    def _():
        for i in range(2):
            for t in range(2):
                kv_far(i, t).wait_send()


def on_device(hidden_rows, norm_gain, w_query, w_key, w_value, w_out, ancestors):
    vmem = pl.BlockSpec(memory_space=pltpu.VMEM)
    hbm = pl.BlockSpec(memory_space=pl.ANY)
    dma = pltpu.SemaphoreType.DMA
    lists = jnp.pad(ancestors, ((0, 0), (0, 128 - MAXA)))
    return pl.pallas_call(
        kernel,
        out_shape=jax.ShapeDtypeStruct((BLOCK, D), BF16),
        in_specs=[vmem, vmem, hbm, hbm, hbm, hbm, hbm, vmem, vmem, vmem, vmem],
        out_specs=vmem,
        scratch_shapes=[
            pltpu.VMEM((4, 2 * BLOCK, D), BF16),
            pltpu.VMEM((D, 2 * HDIM), BF16),
            pltpu.VMEM((D, QCOLS), BF16),
            pltpu.VMEM((QCOLS, D), BF16),
            pltpu.VMEM((4, 2, PER_GROUP, BLOCK, HDIM), BF16),
            pltpu.VMEM((64, 2, BLOCK, HDIM), BF16),
            pltpu.VMEM((4, 2 * BLOCK, QCOLS), BF16),
            pltpu.VMEM((4, BLOCK, D), BF16),
            pltpu.VMEM((2, HALF, D), BF16),
            pltpu.VMEM((2, BLOCK, D), BF16),
            pltpu.VMEM(((MAXA + 1) * BLOCK, HDIM), BF16),
            pltpu.VMEM(((MAXA + 1) * BLOCK, HDIM), BF16),
            pltpu.VMEM((QCOLS, (MAXA + 1) * BLOCK), F32),
            pltpu.VMEM((QCOLS, (MAXA + 1) * BLOCK), BF16),
            pltpu.VMEM((QCOLS, HDIM), F32),
            pltpu.VMEM((8, 128), jnp.int32),
            pltpu.SMEM((2, 8, 128), jnp.int32),
            dma((13,)),
            dma((13,)),
            dma((6,)),
            dma((6, 4)),
            dma((6, 2)),
            dma((4,)),
            dma((34,)),
            dma((32,)),
            dma((20,)),
            dma((20,)),
            dma((1,)),
            dma((1,)),
            dma((2,)),
        ],
        compiler_params=pltpu.CompilerParams(
            collective_id=0, has_side_effects=True, vmem_limit_bytes=60 * 2**20
        ),
        cost_estimate=pl.CostEstimate(
            flops=17 * 10**9, bytes_accessed=20 * 10**6, transcendentals=4 * 10**6
        ),
    )(
        hidden_rows, norm_gain.reshape(1, D), w_query, w_key, w_value, w_out, lists,
        *[jnp.asarray(t) for t in rope_tables()],
    )


def solution(mesh):
    placed = (
        P(("ctx", "head"), None),
        P(),
        P(None, "head"),
        P(None, "head"),
        P(None, "head"),
        P("head", None),
        P("ctx", None),
    )
    return jax.shard_map(
        on_device, mesh=mesh, in_specs=placed, out_specs=P(("ctx", "head"), None), check_vma=False
    )
```

```python
import functools

import jax
import jax.numpy as jnp
import numpy as np
from jax import lax
from jax.experimental import pallas as pl
from jax.experimental.pallas import tpu as pltpu
from jax.sharding import PartitionSpec as P

D = 5120
HDIM = 128
BLOCK = 128
MAXA = 4
PER_GROUP = 5
QCOLS = PER_GROUP * HDIM
HALF = BLOCK // 2
ROPE_BASE = 1000000.0
Q_SCALE = float(HDIM**-0.5 * np.log2(np.e))
MESH = pl.DeviceIdType.MESH
F32 = jnp.float32
BF16 = jnp.bfloat16
N_OUT = 1280
WIDE = D // 2
ROWS = 64


def rope_tables():
    frequency = ROPE_BASE ** (-2.0 * np.arange(HDIM // 2) / HDIM)
    frequency = np.concatenate([frequency, frequency])
    inner = np.arange(BLOCK)[:, None] * frequency[None, :]
    outer = np.arange(128)[:, None] * float(BLOCK) * frequency[None, :]
    return [f(t).astype(np.float32) for t in (inner, outer) for f in (np.cos, np.sin)]


def kernel(
    hid, gain, wq_h, wk_h, wv_h, wo_h, anc_h, ci, si, cb, sb,
    out,
    xb, wkv, wq, wo, qs, kv, att, rb, far, fin, kc, vc, scores, probs, share, anc_v, anc_s,
    ag_s, ag_r, ws_s, ws_r, wz_s, wl, kv_s, kv_r, rs_s, rs_r, an_s, an_r, an_l,
):
    c = lax.axis_index("ctx")
    h = lax.axis_index("head")
    x = h // 2
    par = h % 2
    yh = (c // 2) % 2
    z = c // 4
    k = c % 2
    y = yh * 2 + par
    zp = z % 2
    span = 2 * z + yh
    own = k == par

    def dev(x, y, z, k):
        return {"ctx": z * 4 + (y // 2) * 2 + k, "head": x * 2 + y % 2}

    right = dev((x + 1) % 4, y, z, k)
    left = dev((x + 3) % 4, y, z, k)
    sib = dev(x, y, z, 1 - k)

    def send(src, dst, ssem, rsem, to):
        return pltpu.make_async_remote_copy(
            src_ref=src, dst_ref=dst, send_sem=ssem, recv_sem=rsem, device_id=to, device_id_type=MESH
        )

    barrier = pltpu.get_barrier_semaphore()
    partner = dev(x, yh * 2 + 1 - par, z, k)
    cross_y = (1 - yh) * 2 + 1 - par
    cross = dev(x, cross_y, z, k)
    above = dev(x, y, (z + 1) % 4, k)
    greeted = [right, left, sib, partner, cross, above, dev(x, y, (z + 3) % 4, k)]
    greeted += [dev(x, (y + d) % 4, z, 1 - k) for d in (1, 3)]
    opposite_y = (1 - yh) * 2 + par
    opposite = dev(x, opposite_y, z, k)
    next_z = (z + 3 + 2 * yh) % 4
    greeted += [opposite, dev(x, cross_y, next_z, k), dev(x, opposite_y, next_z, k)]
    for to in greeted:
        pl.semaphore_signal(barrier, 1, device_id=to, device_id_type=MESH)

    local = [
        pltpu.make_async_copy(wk_h, wkv.at[:, pl.ds(0, HDIM)], wl.at[0]),
        pltpu.make_async_copy(wv_h, wkv.at[:, pl.ds(HDIM, HDIM)], wl.at[1]),
        pltpu.make_async_copy(wq_h, wq, wl.at[2]),
        pltpu.make_async_copy(wo_h, wo, wl.at[3]),
    ]

    @pl.when(own)
    def _():
        for copy in local:
            copy.start()

    anc_local = pltpu.make_async_copy(anc_h, anc_s.at[k], an_l.at[0])
    anc_local.start()

    def rows_of(core, first, count):
        return pl.ds(pl.multiple_of(core * BLOCK + first, HALF), count)

    @pl.loop(0, BLOCK // 16)
    def _(i):
        rows = pl.ds(pl.multiple_of(i * 16, 16), 16)
        v = hid[rows, :].astype(F32)
        scale = lax.rsqrt(jnp.mean(v * v, axis=1, keepdims=True) + 1e-06)
        xb[0, pl.ds(pl.multiple_of(k * BLOCK + i * 16, 16), 16), :] = (v * scale * gain[...]).astype(BF16)

    pl.semaphore_wait(barrier, len(greeted))

    A, B = (0, HALF), (HALF, HALF)
    routes = [
        (0, 1, A, right), (0, 1, B, right), (0, 3, B, left), (0, 3, A, left), (0, 0, (0, BLOCK), sib),
        (1, 2, A, right), (3, 2, B, left),
        (1, 1, A, sib), (1, 1, B, sib), (3, 3, B, sib), (3, 3, A, sib), (2, 2, A, sib), (2, 2, B, sib),
    ]

    def ag(m):
        s, t, (first, count), to = routes[m]
        rows = rows_of(k, first, count)
        return send(xb.at[s, rows, :], xb.at[t, rows, :], ag_s.at[m], ag_r.at[m], to)

    for m in range(5):
        ag(m).start()

    anc_send = send(anc_h, anc_v, an_s.at[0], an_r.at[0], sib)
    anc_send.start()

    def chunk(n, quarter):
        def rows(size, part, parts):
            return pl.ds(pl.multiple_of(quarter * size + part * (size // parts), 16), size // parts)

        if n == 0:
            r = rows(D // 4, 0, 1)
            return wk_h.at[r, :], wkv.at[r, pl.ds(0, HDIM)]
        if n == 1:
            r = rows(D // 4, 0, 1)
            return wv_h.at[r, :], wkv.at[r, pl.ds(HDIM, HDIM)]
        if n in (2, 3):
            r = rows(D // 4, n - 2, 2)
            return wq_h.at[r, :], wq.at[r, :]
        r = rows(QCOLS // 4, 0, 1)
        cols = pl.ds((n - 4) * WIDE, WIDE)
        return wo_h.at[r, cols], wo.at[r, cols]

    y_target = dev(x, (y + 3 + 2 * k) % 4, z, par)

    def w_out_send(n):
        quarter = 2 * zp + k
        src, dst = chunk(n, quarter)
        return send(src, dst, ws_s.at[n], ws_r.at[n, quarter], y_target)

    def w_arrival(n, quarter):
        _, dst = chunk(n, quarter)
        return send(dst, dst, ws_s.at[n], ws_r.at[n, quarter], y_target)

    def w_pass(n, side):
        quarter = 2 * zp + side
        _, dst = chunk(n, quarter)
        to = dev(x, y, (z + 1 + 2 * side) % 4, k)
        return send(dst, dst, wz_s.at[n, side], ws_r.at[n, quarter], to)

    def pass_weights(chunks):
        @pl.when(jnp.logical_not(own))
        def _():
            for n in chunks:
                for side in range(2):
                    w_arrival(n, 2 * zp + side).wait_recv()
                    w_pass(n, side).start()

    def wait_weights(chunks, locals_):
        @pl.when(own)
        def _():
            for i in locals_:
                local[i].wait()

        @pl.when(jnp.logical_not(own))
        def _():
            for n in chunks:
                for side in range(2):
                    w_arrival(n, 2 * (1 - zp) + side).wait_recv()

    for n in range(6):
        w_out_send(n).start()

    pass_weights((0, 1))

    def rope(block):
        cos_b, sin_b = cb[pl.ds(block, 1), :], sb[pl.ds(block, 1), :]
        cosine = cos_b * ci[...] - sin_b * si[...]
        sine = sin_b * ci[...] + cos_b * si[...]
        lane = lax.broadcasted_iota(jnp.int32, (BLOCK, HDIM), 1)
        return cosine, jnp.where(lane < HDIM // 2, -sine, sine)

    def rotated(v, table):
        return v * table[0] + pltpu.roll(v, HDIM // 2, 1) * table[1]

    def x_of(r):
        return (x + 4 - r) % 4

    def block_of(r, core):
        return 16 * span + 8 * core + 2 * x_of(r) + par

    def project_kv(r):
        both = jnp.dot(xb[r], wkv[...], preferred_element_type=F32)
        for core in range(2):
            part = both[core * BLOCK : (core + 1) * BLOCK]
            slot = 48 + 8 * par + 2 * x_of(r) + core
            kv[slot, 0] = rotated(part[:, :HDIM], rope(block_of(r, core))).astype(BF16)
            kv[slot, 1] = part[:, HDIM:].astype(BF16)

    def project_q(r):
        for first, count in ((0, 2), (2, 2), (4, 1)):
            got = jnp.dot(xb[r], wq[:, first * HDIM : (first + count) * HDIM], preferred_element_type=F32)
            for core in range(2):
                table = rope(block_of(r, core))
                for e in range(count):
                    part = got[core * BLOCK : (core + 1) * BLOCK, e * HDIM : (e + 1) * HDIM]
                    qs[r, core, first + e] = (rotated(part, table) * Q_SCALE).astype(BF16)

    def kv_pair(region, parity, r):
        return kv.at[pl.ds(16 * region + 8 * parity + 2 * x_of(r), 2)]

    def kv_send(n, src, dst, parity, r, to):
        return send(
            kv_pair(src, parity, r), kv_pair(dst, parity, r), kv_s.at[n], kv_r.at[dst * 8 + parity * 4 + r], to
        )

    def kv_up(r):
        return kv_send(r, 3, 1, par, r, above)

    def kv_partner(r, region):
        return kv_send((16 if region == 1 else 4) + r, region, region, par, r, partner)

    def kv_opposite(region):
        return kv_send(32 + region // 3, region, 2, par, 2, opposite)

    def kv_cross(r, region, mine):
        parity = par if mine else 1 - par
        return kv_send((20 if region == 1 else 8) + 2 * r + mine, region, 2, parity, r, cross)

    def kv_from_partner(r, region):
        return kv_send(0, region, region, 1 - par, r, partner)

    def kv_far(i, t):
        slot = 8 * par + 5 + 2 * i
        to = dev(x, (cross_y, opposite_y)[t], (z + yh) % 4, k)
        return send(
            kv.at[pl.ds(16 + slot, 1)], kv.at[pl.ds(slot, 1)],
            kv_s.at[28 + 2 * i + t], kv_r.at[par * 4 + i], to,
        )

    far_sends = jnp.logical_and(z > 0, z + yh < 4)

    def start_kv(r):
        @pl.when(z < 3)
        def _():
            kv_up(r).start()

        kv_partner(r, 3).start()

        @pl.when(yh == 0)
        def _():
            kv_cross(r, 3, 1).start()
            if r == 2:
                kv_opposite(3).start()

    def pass_kv(r):
        @pl.when(z > 0)
        def _():
            kv_up(r).wait_recv()
            kv_partner(r, 1).start()

            @pl.when(yh == 1)
            def _():
                kv_cross(r, 1, 1).start()
                if r == 2:
                    kv_opposite(1).start()

    def pass_partner_kv(r):
        kv_from_partner(r, 3).wait_recv()

        @pl.when(yh == 0)
        def _():
            kv_cross(r, 3, 0).start()

        @pl.when(z > 0)
        def _():
            kv_from_partner(r, 1).wait_recv()

            @pl.when(yh == 1)
            def _():
                kv_cross(r, 1, 0).start()

    ag(0).wait_recv()
    ag(5).start()
    ag(7).start()
    ag(2).wait_recv()
    ag(6).start()
    ag(9).start()
    pass_weights((2, 3))
    wait_weights((0, 1), (0, 1))
    ag(4).wait_recv()
    project_kv(0)
    start_kv(0)
    ag(1).wait_recv()
    ag(8).start()
    ag(3).wait_recv()
    ag(10).start()
    for m in (7, 8, 9, 10):
        ag(m).wait_recv()

    @pl.loop(0, 2)
    def _(i):
        project_kv(1 + 2 * i)

    for r in (1, 3):
        start_kv(r)
    pass_weights((4,))
    wait_weights((2, 3), (2,))

    project_q(0)
    for r in (0, 1, 3):
        pass_kv(r)
    project_q(1)
    for m in (5, 6):
        ag(m).wait_recv()
        ag(m + 6).start()
    for m in (11, 12):
        ag(m).wait_recv()
    project_kv(2)
    start_kv(2)
    for r in (0, 1, 3):
        pass_partner_kv(r)
    pass_kv(2)

    @pl.when(far_sends)
    def _():
        for i in range(2):
            for t in range(2):
                kv_far(i, t).start()

    pass_weights((5,))

    @pl.loop(2, 4)
    def _(i):
        project_q(i)

    for m in range(13):
        ag(m).wait_send()

    anc_local.wait()
    anc_send.wait()
    anc_move = pltpu.make_async_copy(anc_v, anc_s.at[1 - k], an_l.at[1])
    anc_move.start()
    anc_move.wait()

    def kv_arrival(region, parity, r, blocks):
        ref = kv.at[pl.ds(16 * region + 8 * parity + 2 * r, blocks)]
        return send(ref, ref, kv_s.at[0], kv_r.at[region * 8 + parity * 4 + r], partner)

    kv_from_partner(2, 3).wait_recv()

    @pl.when(z > 0)
    def _():
        kv_from_partner(2, 1).wait_recv()

    @pl.when(span >= 1)
    def _():
        for parity in range(2):
            for r in range(4):
                kv_arrival(2, parity, r, 2).wait_recv()

    @pl.when(span >= 3)
    def _():
        for parity in range(2):
            for i in range(2):
                kv_arrival(0, parity, i, 1).wait_recv()

    def attend(r):
        xr = x_of(r)

        @pl.loop(0, 2)
        def _(core):
            row = 2 * xr + par
            mine = 48 + 8 * par + 2 * xr + core
            kc[0:BLOCK, :] = kv[mine, 0]
            vc[0:BLOCK, :] = kv[mine, 1]
            biases = []
            for j in range(MAXA):
                a = anc_s[core, row, j]
                listed = a >= 0
                place = jnp.where(listed, jnp.clip(a - 16 * span + 48, 0, 63), 48 + 8 * core + row)
                within = place % 16
                slot = (place // 16) * 16 + (within % 2) * 8 + ((within // 2) % 4) * 2 + within // 8
                kc[(j + 1) * BLOCK : (j + 2) * BLOCK, :] = kv[slot, 0]
                vc[(j + 1) * BLOCK : (j + 2) * BLOCK, :] = kv[slot, 1]
                biases.append(jnp.where(listed, 0.0, -1e30).astype(F32))
            q = qs[r, core].reshape(QCOLS, HDIM)
            scores[...] = lax.dot_general(q, kc[...], (((1,), (1,)), ((), ())), preferred_element_type=F32)
            for first in range(0, QCOLS, ROWS):
                rows = slice(first, first + ROWS)
                causal = lax.broadcasted_iota(jnp.int32, (ROWS, BLOCK), 0) + first % BLOCK >= (
                    lax.broadcasted_iota(jnp.int32, (ROWS, BLOCK), 1)
                )
                parts = [jnp.where(causal, scores[rows, 0:BLOCK], -1e30)]
                for j in range(MAXA):
                    parts.append(scores[rows, (j + 1) * BLOCK : (j + 2) * BLOCK] + biases[j])
                top = functools.reduce(jnp.maximum, parts).max(axis=1, keepdims=True)
                parts = [jnp.exp2(part - top) for part in parts]
                total = functools.reduce(jnp.add, parts).sum(axis=1, keepdims=True)
                share[rows, :] = jnp.broadcast_to(1.0 / total, (ROWS, HDIM))
                for j in range(MAXA + 1):
                    probs[rows, j * BLOCK : (j + 1) * BLOCK] = parts[j].astype(BF16)
            mixture = jnp.dot(probs[...], vc[...], preferred_element_type=F32) * share[...]
            for e in range(PER_GROUP):
                att[r, rows_of(core, 0, BLOCK), e * HDIM : (e + 1) * HDIM] = mixture[
                    e * BLOCK : (e + 1) * BLOCK
                ].astype(BF16)

    def wide(j):
        return pl.ds(j * WIDE, WIDE)

    def project_out(r, j):
        @pl.loop(0, WIDE // N_OUT)
        def _(n):
            cols = pl.ds(pl.multiple_of(j * WIDE + n * N_OUT, N_OUT), N_OUT)
            xb[r, :, cols] = jnp.dot(att[r], wo[:, cols], preferred_element_type=F32).astype(BF16)

    def to_sibling(r, j):
        n = 4 * j + r
        src = xb.at[r, rows_of(1 - k, 0, BLOCK), wide(j)]
        return send(src, rb.at[r, :, wide(j)], rs_s.at[n], rs_r.at[n], sib)

    def add_into(r, j, first, count, term):
        @pl.loop(0, count // 16)
        def _(i):
            at = pl.ds(pl.multiple_of(i * 16, 16), 16)
            rows = pl.ds(pl.multiple_of(k * BLOCK + first + i * 16, 16), 16)
            total = xb[r, rows, wide(j)].astype(F32) + term[at, wide(j)].astype(F32)
            xb[r, rows, wide(j)] = total.astype(BF16)

    def half(r, j, first):
        return xb.at[r, rows_of(k, first, HALF), wide(j)]

    def far_send(side, j):
        n = 8 + 2 * j + side
        return send(half(2, j, side * HALF), far.at[side, :, wide(j)], rs_s.at[n], rs_r.at[n], (right, left)[side])

    def fin_send(side, j, first):
        n = 12 + 4 * j + 2 * side + first // HALF
        dst = fin.at[side, pl.ds(first, HALF), wide(j)]
        return send(half((3, 1)[side], j, first), dst, rs_s.at[n], rs_r.at[n], (right, left)[side])

    def take_sibling(r, j):
        to_sibling(r, j).wait_recv()
        add_into(r, j, 0, BLOCK, rb.at[r])

    def put_out(r, j):
        project_out(r, j)
        to_sibling(r, j).start()

    def open_half(j, attend):
        put_out(2, j)
        if j:
            put_out(3, j)
        take_sibling(2, j)
        for side in range(2):
            far_send(side, j).start()
        if not j:
            attend(3)
            put_out(3, j)
        attend(1)
        put_out(1, j)
        take_sibling(3, j)
        fin_send(0, j, HALF).start()
        take_sibling(1, j)
        fin_send(1, j, 0).start()
        attend(0)
        put_out(0, j)

    def close_half(j):
        for side, r, first in ((0, 3, 0), (1, 1, HALF)):
            far_send(side, j).wait_recv()
            add_into(r, j, first, HALF, far.at[side])
            fin_send(side, j, first).start()

    def finish(j):
        to_sibling(0, j).wait_recv()
        for side, first in ((0, HALF), (1, 0), (0, 0), (1, HALF)):
            fin_send(side, j, first).wait_recv()

        @pl.loop(0, BLOCK // 16)
        def _(i):
            at = pl.ds(pl.multiple_of(i * 16, 16), 16)
            rows = pl.ds(pl.multiple_of(k * BLOCK + i * 16, 16), 16)
            total = xb[0, rows, wide(j)].astype(F32) + rb[0, at, wide(j)].astype(F32)
            total = total + fin[0, at, wide(j)].astype(F32) + fin[1, at, wide(j)].astype(F32)
            out[at, wide(j)] = total.astype(BF16)

    attend(2)
    wait_weights((4,), (3,))
    open_half(0, attend)
    close_half(0)
    wait_weights((5,), ())
    open_half(1, lambda r: None)
    close_half(1)
    finish(0)
    finish(1)

    for r in range(4):
        for j in range(2):
            to_sibling(r, j).wait_send()
        kv_partner(r, 3).wait_send()
    for j in range(2):
        for side in range(2):
            far_send(side, j).wait_send()
            for first in (0, HALF):
                fin_send(side, j, first).wait_send()
    for n in range(6):
        w_out_send(n).wait_send()

    @pl.when(jnp.logical_not(own))
    def _():
        for n in range(6):
            for side in range(2):
                w_pass(n, side).wait_send()

    @pl.when(z < 3)
    def _():
        for r in range(4):
            kv_up(r).wait_send()

    @pl.when(yh == 0)
    def _():
        kv_opposite(3).wait_send()
        for r in range(4):
            for mine in range(r == 2, 2):
                kv_cross(r, 3, mine).wait_send()

    @pl.when(z > 0)
    def _():
        for r in range(4):
            kv_partner(r, 1).wait_send()

    @pl.when(jnp.logical_and(z > 0, yh == 1))
    def _():
        kv_opposite(1).wait_send()
        for r in range(4):
            for mine in range(r == 2, 2):
                kv_cross(r, 1, mine).wait_send()

    @pl.when(far_sends)
    def _():
        for i in range(2):
            for t in range(2):
                kv_far(i, t).wait_send()


def on_device(hidden_rows, norm_gain, w_query, w_key, w_value, w_out, ancestors):
    vmem = pl.BlockSpec(memory_space=pltpu.VMEM)
    hbm = pl.BlockSpec(memory_space=pl.ANY)
    dma = pltpu.SemaphoreType.DMA
    lists = jnp.pad(ancestors, ((0, 0), (0, 128 - MAXA)))
    return pl.pallas_call(
        kernel,
        out_shape=jax.ShapeDtypeStruct((BLOCK, D), BF16),
        in_specs=[vmem, vmem, hbm, hbm, hbm, hbm, hbm, vmem, vmem, vmem, vmem],
        out_specs=vmem,
        scratch_shapes=[
            pltpu.VMEM((4, 2 * BLOCK, D), BF16),
            pltpu.VMEM((D, 2 * HDIM), BF16),
            pltpu.VMEM((D, QCOLS), BF16),
            pltpu.VMEM((QCOLS, D), BF16),
            pltpu.VMEM((4, 2, PER_GROUP, BLOCK, HDIM), BF16),
            pltpu.VMEM((64, 2, BLOCK, HDIM), BF16),
            pltpu.VMEM((4, 2 * BLOCK, QCOLS), BF16),
            pltpu.VMEM((4, BLOCK, D), BF16),
            pltpu.VMEM((2, HALF, D), BF16),
            pltpu.VMEM((2, BLOCK, D), BF16),
            pltpu.VMEM(((MAXA + 1) * BLOCK, HDIM), BF16),
            pltpu.VMEM(((MAXA + 1) * BLOCK, HDIM), BF16),
            pltpu.VMEM((QCOLS, (MAXA + 1) * BLOCK), F32),
            pltpu.VMEM((QCOLS, (MAXA + 1) * BLOCK), BF16),
            pltpu.VMEM((QCOLS, HDIM), F32),
            pltpu.VMEM((8, 128), jnp.int32),
            pltpu.SMEM((2, 8, 128), jnp.int32),
            dma((13,)),
            dma((13,)),
            dma((6,)),
            dma((6, 4)),
            dma((6, 2)),
            dma((4,)),
            dma((34,)),
            dma((32,)),
            dma((20,)),
            dma((20,)),
            dma((1,)),
            dma((1,)),
            dma((2,)),
        ],
        compiler_params=pltpu.CompilerParams(
            collective_id=0, has_side_effects=True, vmem_limit_bytes=60 * 2**20
        ),
        cost_estimate=pl.CostEstimate(
            flops=17 * 10**9, bytes_accessed=20 * 10**6, transcendentals=4 * 10**6
        ),
    )(
        hidden_rows, norm_gain.reshape(1, D), w_query, w_key, w_value, w_out, lists,
        *[jnp.asarray(t) for t in rope_tables()],
    )


def solution(mesh):
    placed = (
        P(("ctx", "head"), None),
        P(),
        P(None, "head"),
        P(None, "head"),
        P(None, "head"),
        P("head", None),
        P("ctx", None),
    )
    return jax.shard_map(
        on_device, mesh=mesh, in_specs=placed, out_specs=P(("ctx", "head"), None), check_vma=False
    )
```
